256 devices in a mesh: ctx: 64 (over x, z, core), head: 4 (over y).
Axes of the slice: x: 4, y: 4, z: 8, core: 2. Of those that a mesh axis runs over, the one named last changes fastest.
Arguments:
- hidden: bfloat16 [65536, 1536], P('ctx', 'head'), may hold values from -6 to 6
- norm_gain: float32 [1536], replicated, may hold values from 0.1 to 1.9
- zx_weight: bfloat16 [1536, 2, 3072], P(None, None, 'head'), may hold values from -0.15625 to 0.15625
- bc_weight: bfloat16 [1536, 256], replicated, may hold values from -0.15625 to 0.15625
- dt_weight: bfloat16 [1536, 48], P(None, 'head'), may hold values from -0.15625 to 0.15625
- conv_x: float32 [5, 3072], P(None, 'head'), may hold values from -0.5 to 0.5
- conv_bc: float32 [5, 256], replicated, may hold values from -0.5 to 0.5
- dt_bias: float32 [48], P('head'), may hold values from -4.6 to -2.3
- log_decay: float32 [65536, 48], P('ctx', 'head'), may hold values from -1.5 to 0, as said below
- skip_gain: float32 [48], P('head'), may hold values from 0.5 to 2
- out_gain: float32 [3072], P('head'), may hold values from 0.1 to 1.9
- out_weight: bfloat16 [3072, 1536], P('head'), may hold values from -0.109375 to 0.109375
Outputs:
- mixed: bfloat16 [65536, 1536], P('ctx', 'head')
The draws below stay inside these ranges and needn't reach their ends.
Inputs may be any that keep to these rules, and one draw needn't show every extreme that they name: `log_decay`: negative everywhere; in some heads a token keeps only a few percent of the state after a few tens of positions, other heads decay over the whole document, and a head may lose a sizeable share of its state at single tokens.
All inputs are finite; a program needn't handle non-finite values.
Results may differ from the reference program's by a relative error of at most 0.015.
Values may be sent and summed in bfloat16 or wider, within the bound.
No kernel may reach another device: no remote copies, remote signals or barrier semaphores. Data moves between devices by JAX's collectives and lax.ppermute only.
A program may use at most 128 MiB of HBM per device.

```python
import math
import jax
import jax.numpy as jnp
from jax import lax

D = 1536
HEAD_TOTAL = 48
HEADDIM = 64
STATE = 128
CONV = 4
BLOCK = 256
TOK_DEV = 1024
INNER = 3072
DOCUMENT_LENGTH = 65536
N_HEAD = 4


def draw_log_decay(key, part):
    random_subkeys = jax.random.split(key, 7)
    fast_share = 0.5
    is_fast = jax.random.uniform(random_subkeys[0], (HEAD_TOTAL,)) < fast_share
    fast_rate = 1.0 / jax.random.uniform(random_subkeys[1], (HEAD_TOTAL,), minval=30.0, maxval=50.0)
    slow_rate = jax.random.uniform(random_subkeys[2], (HEAD_TOTAL,), minval=0.2, maxval=0.6) / DOCUMENT_LENGTH
    base_rate = jnp.where(is_fast, fast_rate, slow_rate)
    blocks = DOCUMENT_LENGTH // TOK_DEV
    device_factor = jnp.exp(jax.random.uniform(random_subkeys[3], (blocks, 1, HEAD_TOTAL), minval=-0.4, maxval=0.4))
    token_factor = jnp.exp(jax.random.uniform(random_subkeys[4], (blocks, TOK_DEV, HEAD_TOTAL), minval=-0.7, maxval=0.7))
    decay_speed = (base_rate * device_factor * token_factor).reshape(DOCUMENT_LENGTH, HEAD_TOTAL)
    spike_position = jax.random.randint(random_subkeys[5], (2, HEAD_TOTAL), 0, DOCUMENT_LENGTH)
    spike_magnitude = jnp.log(jax.random.uniform(random_subkeys[6], (2, HEAD_TOTAL), minval=0.5, maxval=0.8))
    token_locations = jnp.arange(DOCUMENT_LENGTH)[:, None]
    spike_events = jnp.where(token_locations == spike_position[0], spike_magnitude[0], 0.0) + jnp.where(token_locations == spike_position[1], spike_magnitude[1], 0.0)
    return (spike_events - decay_speed).astype(jnp.float32)


def levels(rng, shape, cuts, least, top_value):
    def one(dim, parts):
        draws = jax.random.uniform(jax.random.fold_in(jax.random.fold_in(rng, 6), dim), (parts,), jnp.float32, least / len(cuts), top_value / len(cuts))
        return jnp.repeat(jnp.exp(draws), shape[dim] // parts).reshape((-1,) + (1,) * (len(shape) - dim - 1))

    level = one(*cuts[0])
    for cut in cuts[1:]:
        level = level * one(*cut)
    return level


def centred(rng, extent, scale, limit, pieces=(), kind=jnp.bfloat16):
    entries = jax.random.normal(rng, extent, jnp.float32) * scale
    if len(pieces) > 0:
        entries = levels(rng, extent, pieces, -0.22, 0.18) * entries
    return jnp.clip(entries, min=-limit, max=limit).astype(kind)


def setup_inputs(seed: int = 0) -> dict:
    seeds = jax.random.split(jax.random.key(seed), 13)
    return {
        "hidden": centred(seeds[0], (DOCUMENT_LENGTH, D), 1.0, 6.0, ((0, 64), (1, 4))),
        "norm_gain": jnp.clip(1.0 + 0.18 * jax.random.normal(seeds[1], (D,), jnp.float32), 0.1, 1.9),
        "zx_weight": centred(seeds[2], (D, 2, INNER), D ** -0.5, 0.15625, ((2, 4),)),
        "bc_weight": centred(seeds[3], (D, 2 * STATE), D ** -0.5, 0.15625),
        "dt_weight": centred(seeds[4], (D, HEAD_TOTAL), D ** -0.5, 0.15625, ((1, 4),)),
        "conv_x": jnp.clip(jax.random.uniform(seeds[5], (CONV + 1, INNER), jnp.float32, -0.5, 0.5) * levels(seeds[5], (CONV + 1, INNER), ((1, 4),), -0.4, 0.0), -0.5, 0.5),
        "conv_bc": jnp.clip(jax.random.uniform(seeds[6], (CONV + 1, 2 * STATE), jnp.float32, -0.5, 0.5), -0.5, 0.5),
        "dt_bias": jnp.clip(-4.6 + 2.3 * jax.random.uniform(seeds[7], (HEAD_TOTAL,), jnp.float32) ** levels(seeds[7], (HEAD_TOTAL,), ((0, 4),), -0.2, 0.2), -4.6, -2.3),
        "log_decay": draw_log_decay(jax.random.fold_in(seeds[12], 71), 0),
        "skip_gain": jnp.clip(jnp.exp(math.log(2.0) - 1.3862944 * jax.random.uniform(seeds[9], (HEAD_TOTAL,), jnp.float32) ** levels(seeds[9], (HEAD_TOTAL,), ((0, 4),), -0.2, 0.2)), 0.5, 2.0),
        "out_gain": jnp.clip(1.0 + 0.18 * jax.random.normal(seeds[10], (INNER,), jnp.float32), 0.1, 1.9),
        "out_weight": centred(seeds[11], (INNER, D), INNER ** -0.5, 0.109375, ((0, 4),)),
    }


eps = 1e-05

def convolve(extended, conv_taps):
    tap_count = conv_taps.shape[0] - 1
    out_rows = extended.shape[0] - tap_count + 1
    summed_taps = conv_taps[tap_count]
    for offset in range(tap_count):
        summed_taps = summed_taps + conv_taps[offset] * extended[offset:offset + out_rows].astype(jnp.float32)
    return jax.nn.silu(summed_taps).astype(jnp.bfloat16)

def reference(hidden, norm_gain, zx_weight, bc_weight, dt_weight, conv_x, conv_bc, dt_bias, log_decay, skip_gain, out_gain, out_weight):
    rim_rows = CONV - 1
    position = jnp.arange(BLOCK)
    causal = position[:, None] >= position[None, :]
    group_width = INNER // N_HEAD
    highest = lax.Precision.HIGHEST

    def advance(carry_in, block_in):
        previous_raw, state = carry_in
        row_block, decay_rows = block_in
        values = row_block.astype(jnp.float32)
        mean_square = lax.optimization_barrier(jnp.mean(values * values, axis=-1, keepdims=True))
        normed = (values * lax.rsqrt(mean_square + eps) * norm_gain).astype(jnp.bfloat16)
        gate_raw = jnp.dot(normed, zx_weight[:, 0, :], preferred_element_type=jnp.float32).astype(jnp.bfloat16)
        x_raw = jnp.dot(normed, zx_weight[:, 1, :], preferred_element_type=jnp.float32).astype(jnp.bfloat16)
        bc_raw = jnp.dot(normed, bc_weight, preferred_element_type=jnp.float32).astype(jnp.bfloat16)
        step_raw = jnp.dot(normed, dt_weight, preferred_element_type=jnp.float32).astype(jnp.bfloat16)
        projected = jnp.concatenate([x_raw, bc_raw], axis=1)
        extended = jnp.concatenate([previous_raw, projected], axis=0)
        x_conv = convolve(extended[:, :INNER], conv_x)
        bc_conv = convolve(extended[:, INNER:], conv_bc)
        b_rows = bc_conv[:, :STATE]
        c_rows = bc_conv[:, STATE:]
        step_size = jax.nn.softplus(step_raw.astype(jnp.float32) + dt_bias)
        decay_sum = jnp.cumsum(decay_rows, axis=0)
        decay_t = decay_sum.T
        step_t = step_size.T
        scores = jnp.dot(c_rows, b_rows.T, preferred_element_type=jnp.float32)
        log_gap = jnp.where(causal, decay_t[:, :, None] - decay_t[:, None, :], 0.0)
        mix_weights = jnp.where(causal, scores[None] * jnp.exp(log_gap) * step_t[:, None, :], 0.0).astype(jnp.bfloat16)
        x_heads = x_conv.reshape(BLOCK, HEAD_TOTAL, HEADDIM).astype(jnp.float32)
        y_inside = jnp.einsum('hts,shp->thp', mix_weights.astype(jnp.float32), x_heads, precision=highest)
        c_wide = c_rows.astype(jnp.float32)
        b_wide = b_rows.astype(jnp.float32)
        y_carried = jnp.exp(decay_sum)[:, :, None] * jnp.einsum('tn,hpn->thp', c_wide, state, precision=highest)
        to_end = jnp.exp(decay_t[:, -1:] - decay_t) * step_t
        weighted = x_heads * to_end.T[:, :, None]
        block_state = jnp.einsum('shp,sn->hpn', weighted, b_wide, precision=highest)
        new_state = jnp.exp(decay_t[:, -1])[:, None, None] * state + block_state
        y_heads = y_inside + y_carried + skip_gain[None, :, None] * x_heads
        gated = y_heads.reshape(BLOCK, INNER) * jax.nn.silu(gate_raw.astype(jnp.float32))
        square_mean = lax.optimization_barrier(jnp.mean(gated * gated, axis=-1, keepdims=True))
        y_normed = (gated * lax.rsqrt(square_mean + eps) * out_gain).astype(jnp.bfloat16)
        summed = jnp.zeros((BLOCK, D), jnp.float32)
        for group in range(N_HEAD):
            piece = jnp.dot(y_normed[:, group * group_width:(group + 1) * group_width], out_weight[group * group_width:(group + 1) * group_width], preferred_element_type=jnp.float32).astype(jnp.bfloat16)
            piece = lax.optimization_barrier(piece)
            summed = summed + piece.astype(jnp.float32)
        return ((extended[extended.shape[0] - rim_rows:], new_state), summed.astype(jnp.bfloat16))
    start_carry = (jnp.zeros((rim_rows, INNER + 2 * STATE), jnp.bfloat16), jnp.zeros((HEAD_TOTAL, HEADDIM, STATE), jnp.float32))
    block_total = DOCUMENT_LENGTH // BLOCK
    unused, outputs = lax.scan(advance, start_carry, (hidden.reshape(block_total, BLOCK, D), log_decay.reshape(block_total, BLOCK, HEAD_TOTAL)))
    return outputs.reshape(DOCUMENT_LENGTH, D)
```

```python
import functools
import jax
import jax.numpy as jnp
from jax import lax
from jax.experimental import pallas as pl
from jax.experimental.pallas import tpu as pltpu
from jax.sharding import PartitionSpec as P

HEADDIM = 64
STATE = 128
CONV = 4
BLOCK = 256
INNER = 3072
D = 1536
LANES = 128
RIM = 8
eps = 1e-05
f32 = jnp.float32
bf16 = jnp.bfloat16


def split(v):
    hi = v.astype(bf16)
    return jnp.concatenate([hi, (v - hi.astype(f32)).astype(bf16)], axis=1)


def silu(v):
    return v / (1.0 + jnp.exp(-v))


def front_kernel(
    inner, last,
    acc, piece, gain, weight, squares, rim, state_in, taps, dt_bias, to_end, spread, keep, total,
    gate, x_out, bc_out, xs_out, entering, state, tail, payload, extended, slabs,
):
    index = pl.program_id(0)
    wide = inner + 2 * STATE

    @pl.when(index == 0)
    def _():
        extended[0:RIM] = rim[...]
        state[...] = state_in[...]

    @pl.when(index > 0)
    def _():
        extended[0:RIM] = extended[BLOCK : BLOCK + RIM]

    values = piece[...].astype(f32)
    square = squares[...] + jnp.sum(values * values, axis=1, keepdims=True)
    scale = lax.rsqrt(square * (1.0 / D) + eps)
    full = acc[...] + jnp.dot(
        (values * gain[...]).astype(bf16), weight[...], preferred_element_type=f32
    )
    raw = (full * scale).astype(bf16)
    gate[...] = raw[:, :inner]
    extended[RIM : RIM + BLOCK] = raw[:, inner : inner + wide].astype(f32)
    step = jax.nn.softplus(raw[:, inner + wide :].astype(f32) + dt_bias[...])
    summed = taps[CONV : CONV + 1]
    for k in range(CONV):
        first = RIM - CONV + 1 + k
        summed = summed + taps[k : k + 1] * extended[first : first + BLOCK]
    conv = silu(summed)
    x_conv = conv[:, :inner].astype(bf16)
    bc = conv[:, inner:].astype(bf16)
    x_out[...] = x_conv
    bc_out[...] = bc
    x_wide = x_conv.astype(f32)
    by_step = jnp.dot(split(step), spread[...], preferred_element_type=f32)
    by_end = jnp.dot(split(step * to_end[...]), spread[...], preferred_element_type=f32)
    xs_out[...] = (x_wide * by_step).astype(bf16)
    weighted = (x_wide * by_end).astype(bf16)
    entering[0] = state[...]
    state[...] = keep[0] * state[...] + lax.dot_general(
        bc[:, :STATE], weighted, (((0,), (0,)), ((), ())), preferred_element_type=f32
    )

    @pl.when(index == pl.num_programs(0) - 1)
    def _():
        tail[...] = extended[BLOCK : BLOCK + RIM]
        if last:
            half = STATE // 2
            chunks = inner // LANES
            slabs[...] = jnp.zeros_like(slabs)
            for c in range(chunks):
                slabs[:, c] = state[0:half, c * LANES : (c + 1) * LANES]
                slabs[:, chunks + c] = state[half:STATE, c * LANES : (c + 1) * LANES]
            slabs[:, 2 * chunks] = jnp.broadcast_to(total[...], (half, LANES))
            payload[...] = slabs[...].astype(bf16)
        else:
            payload[...] = jnp.zeros_like(payload)


def front(last, acc, piece, gain, weight, squares, rim, state_in, taps, dt_bias, to_end, spread, keep, total, half):
    rows = acc.shape[0]
    inner = state_in.shape[1]
    grid = rows // BLOCK
    base = half * grid

    def row(width, offset=0):
        return pl.BlockSpec((BLOCK, width), lambda i: (i + offset, 0))

    def whole(*shape):
        return pl.BlockSpec(shape, lambda i: (0,) * len(shape))

    wide = inner + 2 * STATE
    pieces = STATE // 2
    return pl.pallas_call(
        functools.partial(front_kernel, inner, last),
        grid=(grid,),
        in_specs=[
            row(acc.shape[1]), row(piece.shape[1]), whole(*gain.shape), whole(*weight.shape),
            row(1), whole(RIM, wide), whole(STATE, inner), whole(CONV + 1, wide),
            whole(1, LANES), row(LANES, base), whole(2 * LANES, inner),
            pl.BlockSpec((1, 1, inner), lambda i: (i + base, 0, 0)), whole(1, LANES),
        ],
        out_specs=[
            row(inner), row(inner), row(2 * STATE), row(inner),
            pl.BlockSpec((1, STATE, inner), lambda i: (i, 0, 0)),
            whole(STATE, inner), whole(RIM, wide), whole(pieces, 16, LANES),
        ],
        out_shape=[
            jax.ShapeDtypeStruct((rows, inner), bf16),
            jax.ShapeDtypeStruct((rows, inner), bf16),
            jax.ShapeDtypeStruct((rows, 2 * STATE), bf16),
            jax.ShapeDtypeStruct((rows, inner), bf16),
            jax.ShapeDtypeStruct((grid, STATE, inner), f32),
            jax.ShapeDtypeStruct((STATE, inner), f32),
            jax.ShapeDtypeStruct((RIM, wide), f32),
            jax.ShapeDtypeStruct((pieces, 16, LANES), bf16),
        ],
        scratch_shapes=[
            pltpu.VMEM((BLOCK + RIM, wide), f32),
            pltpu.VMEM((pieces, 16, LANES), f32),
        ],
        compiler_params=pltpu.CompilerParams(vmem_limit_bytes=40 * 2**20),
        cost_estimate=pl.CostEstimate(
            flops=2 * rows * piece.shape[1] * acc.shape[1] * 2,
            bytes_accessed=rows * acc.shape[1] * 6, transcendentals=rows * wide,
        ),
        name="front",
    )(acc, piece, gain, weight, squares, rim, state_in, taps, dt_bias, to_end, spread, keep, total)


def scan_kernel(chunks, taken, spread, given, decays, sums):
    count = taken.shape[0]
    wide = taken[...].astype(f32)
    decays[...] = wide
    rows = decays[:, 2 * chunks]
    gains = jnp.exp(jnp.dot(rows.astype(bf16), spread[...], preferred_element_type=f32))
    sums[...] = wide
    decays[...] = jnp.zeros_like(decays)
    for c in range(chunks):
        part = gains[:, c * LANES : (c + 1) * LANES]
        decays[:, c] = part
        decays[:, chunks + c] = part
    running = jnp.zeros(taken.shape[1:], f32)
    for j in range(count):
        following = decays[j] * running + sums[j]
        sums[j] = running
        running = following
    given[...] = sums[...].astype(bf16)


def scan(taken, spread):
    chunks = spread.shape[1] // LANES
    return pl.pallas_call(
        functools.partial(scan_kernel, chunks),
        out_shape=jax.ShapeDtypeStruct(taken.shape, bf16),
        scratch_shapes=[pltpu.VMEM(taken.shape, f32), pltpu.VMEM(taken.shape, f32)],
        name="scan",
    )(taken, spread)


def inside_kernel(heads, bc, xs, decay, decay_t, out):
    both = bc[...]
    scores = lax.dot_general(
        both[:, STATE:], both[:, :STATE], (((1,), (1,)), ((), ())), preferred_element_type=f32
    )
    row = lax.broadcasted_iota(jnp.int32, (BLOCK, BLOCK), 0)
    column = lax.broadcasted_iota(jnp.int32, (BLOCK, BLOCK), 1)
    scores = jnp.where(row >= column, scores, 0.0)
    sums = decay[...]
    first = lax.broadcasted_iota(jnp.int32, (BLOCK, LANES), 1) < HEADDIM
    for pair in range(heads // 2):
        span = slice(pair * LANES, (pair + 1) * LANES)
        found = []
        for h in (2 * pair, 2 * pair + 1):
            gap = jnp.minimum(sums[:, h : h + 1] - decay_t[h : h + 1, :], 0.0)
            mix = (scores * jnp.exp(gap)).astype(bf16)
            found.append(jnp.dot(mix, xs[:, span], preferred_element_type=f32))
        out[:, span] = jnp.where(first, found[0], found[1])


def inside(bc, xs, decay, decay_t, half):
    rows, inner = xs.shape
    grid = rows // BLOCK
    base = half * grid
    return pl.pallas_call(
        functools.partial(inside_kernel, inner // HEADDIM),
        grid=(grid,),
        in_specs=[
            pl.BlockSpec((BLOCK, 2 * STATE), lambda i: (i, 0)),
            pl.BlockSpec((BLOCK, inner), lambda i: (i, 0)),
            pl.BlockSpec((BLOCK, LANES), lambda i: (i + base, 0)),
            pl.BlockSpec((16, BLOCK), lambda i: (0, i + base)),
        ],
        out_specs=pl.BlockSpec((BLOCK, inner), lambda i: (i, 0)),
        out_shape=jax.ShapeDtypeStruct((rows, inner), f32),
        compiler_params=pltpu.CompilerParams(vmem_limit_bytes=32 * 2**20),
        cost_estimate=pl.CostEstimate(
            flops=2 * rows * BLOCK * inner * 4, bytes_accessed=rows * inner * 6,
            transcendentals=rows * BLOCK * inner // HEADDIM,
        ),
        name="inside",
    )(bc, xs, decay, decay_t)


def tail_kernel(
    inner,
    y_in, x_conv, gate, bc, entering, taken, before, decay, spread, skip, gain, weight,
    far, right, left, own, squares, slabs, incoming,
):
    chunks = inner // LANES

    @pl.when(pl.program_id(0) == 0)
    def _():
        slabs[...] = taken[...].astype(f32)
        half = STATE // 2
        for c in range(chunks):
            incoming[0:half, c * LANES : (c + 1) * LANES] = slabs[:, c]
            incoming[half:STATE, c * LANES : (c + 1) * LANES] = slabs[:, chunks + c]

    carried = (entering[0] + before[0] * incoming[...]).astype(bf16)
    fade = jnp.dot(split(jnp.exp(decay[...])), spread[...], preferred_element_type=f32)
    y = y_in[...] + fade * jnp.dot(bc[:, STATE:], carried, preferred_element_type=f32)
    y = y + skip[...] * x_conv[...].astype(f32)
    gated = y * silu(gate[...].astype(f32))
    squares[...] = jnp.sum(gated * gated, axis=1, keepdims=True)
    scaled = (gated * gain[...]).astype(bf16)
    width = far.shape[1]
    for n, out in enumerate((own, right, far, left)):
        out[...] = jnp.dot(
            scaled, weight[:, n * width : (n + 1) * width], preferred_element_type=f32
        ).astype(bf16)


def tail(y_in, x_conv, gate, bc, entering, taken, before, decay, spread, skip, gain, weight, half):
    rows, inner = y_in.shape
    grid = rows // BLOCK
    base = half * grid
    width = weight.shape[1] // 4

    def row(width, offset=0):
        return pl.BlockSpec((BLOCK, width), lambda i: (i + offset, 0))

    def whole(*shape):
        return pl.BlockSpec(shape, lambda i: (0,) * len(shape))

    return pl.pallas_call(
        functools.partial(tail_kernel, inner),
        grid=(grid,),
        in_specs=[
            row(inner), row(inner), row(inner), row(2 * STATE),
            pl.BlockSpec((1, STATE, inner), lambda i: (i, 0, 0)),
            whole(*taken.shape),
            pl.BlockSpec((1, 1, inner), lambda i: (i + base, 0, 0)),
            row(LANES, base), whole(2 * LANES, inner), whole(1, inner), whole(1, inner),
            whole(*weight.shape),
        ],
        out_specs=[row(width)] * 4 + [row(1)],
        out_shape=[jax.ShapeDtypeStruct((rows, width), bf16)] * 4
        + [jax.ShapeDtypeStruct((rows, 1), f32)],
        scratch_shapes=[pltpu.VMEM(taken.shape, f32), pltpu.VMEM((STATE, inner), f32)],
        compiler_params=pltpu.CompilerParams(vmem_limit_bytes=40 * 2**20),
        cost_estimate=pl.CostEstimate(
            flops=2 * rows * inner * weight.shape[1] + 2 * rows * inner * STATE,
            bytes_accessed=rows * inner * 10 + weight.size * 2, transcendentals=rows * inner,
        ),
        name="tail",
    )(y_in, x_conv, gate, bc, entering, taken, before, decay, spread, skip, gain, weight)


def per_device(
    hidden, norm_gain, zx_weight, bc_weight, dt_weight, conv_x, conv_bc, dt_bias,
    log_decay, skip_gain, out_gain, out_weight,
):
    rows, width = hidden.shape
    heads = dt_weight.shape[1]
    inner = zx_weight.shape[2]
    blocks = rows // BLOCK
    middle = rows // 2
    groups = lax.axis_size("head")
    places = lax.axis_size("ctx")
    me = lax.axis_index("head")
    to_right = [(i, (i + 1) % groups) for i in range(groups)]
    to_left = [(i, (i - 1) % groups) for i in range(groups)]

    def right(v):
        return lax.ppermute(v, "head", to_right)

    def left(v):
        return lax.ppermute(v, "head", to_left)

    top, bottom = hidden[:middle], hidden[middle:]
    right_top, left_bottom = right(top), left(bottom)
    right_bottom, left_top = right(bottom), left(top)
    far_top, far_bottom = right(right_top), left(left_bottom)

    rim_rows = lax.ppermute(
        hidden[rows - RIM :], "ctx", [(i, i + 1) for i in range(places - 1)]
    )
    rim_rows = lax.all_gather(rim_rows, "head", axis=1, tiled=True)

    weights = jnp.concatenate(
        [
            zx_weight.reshape(D, 2 * inner),
            bc_weight,
            jnp.pad(dt_weight, ((0, 0), (0, LANES - heads))),
        ],
        axis=1,
    )
    by_owner = weights.reshape(groups, width, weights.shape[1])
    gains = norm_gain.reshape(groups, 1, width)

    def owned(array, offset):
        return lax.dynamic_index_in_dim(array, lax.rem(me + offset, groups), 0, False)

    def product(piece, offset):
        wide = piece.astype(f32)
        return (
            jnp.dot(
                (wide * owned(gains, offset)).astype(bf16),
                owned(by_owner, offset),
                preferred_element_type=f32,
            ),
            jnp.sum(wide * wide, axis=1, keepdims=True),
        )

    def gathered(own, from_left, from_right):
        a, sa = product(own, 0)
        b, sb = product(from_left, groups - 1)
        c, sc = product(from_right, 1)
        return a + b + c, sa + sb + sc

    acc_top, squares_top = gathered(top, right_top, left_top)
    acc_bottom, squares_bottom = gathered(bottom, right_bottom, left_bottom)

    rim_wide = rim_rows.astype(f32)
    rim_scale = lax.rsqrt(jnp.mean(rim_wide * rim_wide, axis=1, keepdims=True) + eps)
    rim = (
        jnp.dot(
            (rim_wide * norm_gain).astype(bf16),
            weights[:, inner : 2 * inner + 2 * STATE],
            preferred_element_type=f32,
        )
        * rim_scale
    ).astype(bf16).astype(f32)

    lower = (jnp.arange(BLOCK)[:, None] >= jnp.arange(BLOCK)[None, :]).astype(f32)
    sums = jnp.einsum(
        "ts,bsh->bth", lower, log_decay.reshape(blocks, BLOCK, heads),
        precision=lax.Precision.HIGHEST,
    )
    totals = sums[:, -1]
    lanes = ((0, 0), (0, LANES - heads))
    decay = jnp.pad(sums.reshape(rows, heads), lanes)
    decay_t = jnp.pad(jnp.transpose(sums.reshape(rows, heads)), ((0, 16 - heads), (0, 0)))
    to_end = jnp.pad(jnp.exp(totals[:, None] - sums).reshape(rows, heads), lanes)
    head_of = jnp.arange(inner) // HEADDIM
    one_hot = (jnp.arange(LANES)[:, None] == head_of[None, :]).astype(bf16)
    spread = jnp.concatenate([one_hot, one_hot], axis=0)
    lane = jnp.arange(LANES)
    thrice = (
        ((lane % heads)[:, None] == head_of[None, :]) & (lane < 3 * heads)[:, None]
    ).astype(bf16)
    keep = jnp.repeat(jnp.exp(totals), HEADDIM, axis=1)[:, None]
    ahead = [jnp.zeros_like(totals[0])]
    for k in range(blocks):
        ahead.append(ahead[-1] + totals[k])
    before = jnp.repeat(jnp.exp(jnp.stack(ahead[:blocks])), HEADDIM, axis=1)[:, None]
    whole = ahead[blocks]
    high = lax.reduce_precision(whole, 8, 7)
    mid = lax.reduce_precision(whole - high, 8, 7)
    low = whole - high - mid
    total = jnp.pad(jnp.concatenate([high, mid, low]), (0, LANES - 3 * heads))[None]

    taps = jnp.concatenate([conv_x, conv_bc], axis=1)
    bias = jnp.pad(dt_bias, (0, LANES - heads))[None]
    far_gain, far_weight = owned(gains, 2), owned(by_owner, 2)

    zero = jnp.zeros((STATE, inner), f32)
    gate_a, x_a, bc_a, xs_a, enter_a, state_a, rim_a, _ = front(
        False, acc_top, far_top, far_gain, far_weight, squares_top, rim, zero,
        taps, bias, to_end, spread, keep, total, 0,
    )
    gate_b, x_b, bc_b, xs_b, enter_b, _, _, payload = front(
        True, acc_bottom, far_bottom, far_gain, far_weight, squares_bottom, rim_a, state_a,
        taps, bias, to_end, spread, keep, total, 1,
    )
    taken = lax.all_to_all(payload, "ctx", 0, 0)
    incoming = lax.all_to_all(scan(taken, thrice), "ctx", 0, 0)
    inside_a = inside(bc_a, xs_a, decay, decay_t, 0)
    inside_b = inside(bc_b, xs_b, decay, decay_t, 1)

    turned = jnp.concatenate(
        [
            lax.dynamic_slice_in_dim(out_weight, lax.rem(me + k, groups) * width, width, 1)
            for k in range(groups)
        ],
        axis=1,
    )
    skip = jnp.repeat(skip_gain, HEADDIM)[None]
    gain = out_gain[None]
    far_a, right_a, left_a, own_a, sq_a = tail(
        inside_a, x_a, gate_a, bc_a, enter_a, incoming, before, decay, spread, skip, gain,
        turned, 0,
    )
    far_b, right_b, left_b, own_b, sq_b = tail(
        inside_b, x_b, gate_b, bc_b, enter_b, incoming, before, decay, spread, skip, gain,
        turned, 1,
    )

    def add(u, v):
        return (u.astype(f32) + v.astype(f32)).astype(bf16)

    passed_a, direct_a = right(far_a), left(left_a)
    passed_b, direct_b = left(far_b), right(right_b)
    arrived_a = right(add(right_a, passed_a))
    arrived_b = left(add(left_b, passed_b))
    squares = lax.psum(
        jnp.concatenate([sq_a.reshape(-1, LANES), sq_b.reshape(-1, LANES)], axis=0), "head"
    )
    scale = lax.rsqrt(squares / INNER + eps).reshape(rows, 1)
    total_a = own_a.astype(f32) + direct_a.astype(f32) + arrived_a.astype(f32)
    total_b = own_b.astype(f32) + direct_b.astype(f32) + arrived_b.astype(f32)
    return jnp.concatenate(
        [(total_a * scale[:middle]).astype(bf16), (total_b * scale[middle:]).astype(bf16)], axis=0
    )


def solution(mesh):
    placed = (
        P("ctx", "head"), P(), P(None, None, "head"), P(), P(None, "head"), P(None, "head"), P(),
        P("head"), P("ctx", "head"), P("head"), P("head"), P("head", None),
    )
    return jax.shard_map(
        per_device, mesh=mesh, in_specs=placed, out_specs=P("ctx", "head"), check_vma=False
    )
```

```python
import functools
import jax
import jax.numpy as jnp
from jax import lax
from jax.experimental import pallas as pl
from jax.experimental.pallas import tpu as pltpu
from jax.sharding import PartitionSpec as P

HEADDIM = 64
STATE = 128
CONV = 4
BLOCK = 256
INNER = 3072
D = 1536
LANES = 128
RIM = 16
VMEM = 24 * 2**20
LIGHT = pl.CostEstimate(flops=1024, bytes_accessed=1024, transcendentals=0)
eps = 1e-05
f32 = jnp.float32
bf16 = jnp.bfloat16


def kept(*arrays):
    return [pltpu.with_memory_space_constraint(v, pltpu.HBM) for v in arrays]


def far_memory(shape, kind):
    return pltpu.HBM(shape, kind)


def split(v):
    hi = v.astype(bf16)
    return jnp.concatenate([hi, (v - hi.astype(f32)).astype(bf16)], axis=1)


def coded(v):
    hi = v.astype(bf16).astype(f32)
    return jnp.concatenate([hi, v - hi], axis=0).astype(bf16)


def decoded(v):
    wide = v.astype(f32)
    return wide[:8] + wide[8:]


def silu(v):
    return 0.5 * v * (1.0 + jnp.tanh(0.5 * v))


def prepare_kernel(
    heads, inner, blocks,
    log_decay_t, dt_t, bc_weight, conv_x, conv_bc, dt_bias, skip_gain,
    decay, decay_t, to_end, channels, total, spread, thrice, others, taps, bias,
):
    lower = lax.broadcasted_iota(jnp.int32, (BLOCK, BLOCK), 0)
    upper = lax.broadcasted_iota(jnp.int32, (BLOCK, BLOCK), 1)
    ones = (lower <= upper).astype(f32)
    highest = lax.Precision.HIGHEST

    def dot(u, v):
        return jnp.dot(u, v, preferred_element_type=f32, precision=highest)

    def tall(v):
        padded = jnp.concatenate([v, jnp.zeros((LANES - heads, v.shape[1]), f32)], axis=0)
        return jnp.transpose(padded)

    lanes = lax.broadcasted_iota(jnp.int32, (LANES, inner), 0)
    head_of = lax.broadcasted_iota(jnp.int32, (LANES, inner), 1) // HEADDIM
    one_hot = (lanes == head_of).astype(f32)
    spread[0:LANES] = one_hot.astype(bf16)
    spread[LANES:] = one_hot.astype(bf16)
    three = (lanes == head_of) | (lanes == head_of + heads) | (lanes == head_of + 2 * heads)
    thrice[...] = three.astype(f32).astype(bf16)
    decay_t[...] = jnp.zeros_like(decay_t)
    totals = []
    for k in range(blocks):
        span = slice(k * BLOCK, (k + 1) * BLOCK)
        sums_t = dot(log_decay_t[:, span], ones)
        decay_t[0:heads, span] = sums_t
        sums = tall(sums_t)
        decay[span] = sums
        last = sums[BLOCK - 1 : BLOCK]
        to_end[span] = jnp.exp(last - sums)
        totals.append(last)
    rows = [jnp.exp(v) for v in totals]
    fades = []
    for h in range(2):
        passed = jnp.zeros((1, LANES), f32)
        for k in range(blocks // 2):
            rows.append(jnp.exp(passed))
            passed = passed + totals[h * (blocks // 2) + k]
        fades.append(passed)
    rows += [jnp.exp(v) for v in fades]

    def row(v):
        return jnp.concatenate([v, jnp.zeros((1, LANES - heads), f32)], axis=1)

    rows.append(row(skip_gain[...]))
    rows.append(jnp.ones((1, LANES), f32))
    while len(rows) < 16:
        rows.append(jnp.zeros((1, LANES), f32))
    channels[...] = dot(jnp.concatenate(rows, axis=0), one_hot)
    whole = fades[0] + fades[1]
    high = whole.astype(bf16).astype(f32)
    mid = (whole - high).astype(bf16).astype(f32)
    low = whole - high - mid
    total[...] = jnp.concatenate(
        [high[:, :heads], mid[:, :heads], low[:, :heads], jnp.zeros((1, LANES - 3 * heads), f32)], axis=1
    )
    bias[...] = row(dt_bias[...])
    others[:, : 2 * STATE] = bc_weight[...]
    others[:, 2 * STATE :] = tall(dt_t[...].astype(f32)).astype(bf16)
    taps[0 : CONV + 1, :inner] = conv_x[...]
    taps[0 : CONV + 1, inner:] = conv_bc[...]


def prepare(log_decay_t, dt_t, bc_weight, conv_x, conv_bc, dt_bias, skip_gain):
    heads, rows = log_decay_t.shape
    inner = conv_x.shape[1]
    blocks = rows // BLOCK
    shapes = [
        ((rows, LANES), f32), ((16, rows), f32), ((rows, LANES), f32), ((16, inner), f32),
        ((1, LANES), f32), ((2 * LANES, inner), bf16), ((LANES, inner), bf16),
        ((D, 2 * STATE + LANES), bf16), ((CONV + 1, inner + 2 * STATE), f32), ((1, LANES), f32),
    ]
    return pl.pallas_call(
        functools.partial(prepare_kernel, heads, inner, blocks),
        out_shape=[jax.ShapeDtypeStruct(*v) for v in shapes],
        compiler_params=pltpu.CompilerParams(vmem_limit_bytes=VMEM),
        cost_estimate=LIGHT,
        name="prepare",
    )(log_decay_t, dt_t, bc_weight, conv_x, conv_bc, dt_bias, skip_gain)


def gather_kernel(
    owners, own, from_left, from_right, gain_0, gain_1, gain_2, w_0, w_1, w_2, o_0, o_1, o_2,
    acc, acc_others, squares, lhs,
):
    width = own.shape[1]
    step = pl.program_id(0)

    @pl.when(step == 0)
    def _():
        square = None
        for k, (piece, gain) in enumerate(((own, gain_0), (from_left, gain_1), (from_right, gain_2))):
            values = piece[...].astype(f32)
            lhs[:, k * width : (k + 1) * width] = (values * gain[0]).astype(bf16)
            part = jnp.sum(values * values, axis=1, keepdims=True)
            square = part if square is None else square + part
        squares[...] = square

    acc[0] = jnp.dot(
        lhs[...], jnp.concatenate([w_0[0], w_1[0], w_2[0]], axis=0), preferred_element_type=f32
    )

    @pl.when(step == 1)
    def _():
        acc_others[...] = jnp.dot(
            lhs[...], jnp.concatenate([o_0[...], o_1[...], o_2[...]], axis=0),
            preferred_element_type=f32,
        )


def gather(owners, own, from_left, from_right, gains, gate_x, others):
    rows, width = own.shape
    inner = gate_x.shape[2]
    narrow = others.shape[1]

    def whole(*shape):
        return pl.BlockSpec(shape, lambda n, o: (0,) * len(shape))

    def gain(k):
        return pl.BlockSpec((1, 1, width), lambda n, o: (o[k], 0, 0))

    def wide(k):
        return pl.BlockSpec((1, width, inner), lambda n, o: (n, o[k], 0))

    def small(k):
        return pl.BlockSpec((width, narrow), lambda n, o: (o[k], 0))

    return pl.pallas_call(
        gather_kernel,
        grid_spec=pltpu.PrefetchScalarGridSpec(
            num_scalar_prefetch=1,
            grid=(2,),
            in_specs=[whole(rows, width)] * 3 + [f(k) for f in (gain, wide, small) for k in range(3)],
            out_specs=[
                pl.BlockSpec((1, rows, inner), lambda n, o: (n, 0, 0)), whole(rows, narrow), whole(rows, 1),
            ],
            scratch_shapes=[pltpu.VMEM((rows, 3 * width), bf16)],
        ),
        out_shape=[
            far_memory((2, rows, inner), f32), far_memory((rows, narrow), f32), far_memory((rows, 1), f32),
        ],
        compiler_params=pltpu.CompilerParams(vmem_limit_bytes=VMEM),
        cost_estimate=LIGHT,
        name="gather",
    )(owners, own, from_left, from_right, gains, gains, gains, gate_x, gate_x, gate_x, others, others, others)


def front_kernel(
    inner, last,
    owner, acc, acc_others, piece, squares, gain, gate_x, others, near, taps, dt_bias, to_end, spread, keep, total,
    *rest,
):
    if last:
        later, join, gate, x_out, bc_out, xs_out, entering, state, payload, extended, slabs = rest
    else:
        rim_acc, rim_others, rim_piece, rim_squares, gate, x_out, bc_out, xs_out, entering, state, tail, extended = rest
    index = pl.program_id(0)
    wide = inner + 2 * STATE

    def scaled(piece):
        values = piece[...].astype(f32)
        return values, (values * gain[0]).astype(bf16)

    def row_scale(squares, values):
        square = squares[...] + jnp.sum(values * values, axis=1, keepdims=True)
        return lax.rsqrt(square * (1.0 / D) + eps)

    def dot(u, v):
        return jnp.dot(u, v, preferred_element_type=f32)

    @pl.when(index == 0)
    def _():
        state[...] = jnp.zeros_like(state)
        if last:
            extended[0:RIM] = near[...].astype(f32)
        else:
            values, lhs = scaled(rim_piece)
            scale = row_scale(rim_squares, values)
            x_rim = (rim_acc[1] + dot(lhs, gate_x[1])) * scale
            bc_rim = (
                rim_others[:, : 2 * STATE] + dot(lhs, others[:, : 2 * STATE])
            ) * scale
            extended[0:RIM, :inner] = x_rim.astype(bf16).astype(f32)
            extended[0:RIM, inner:] = bc_rim.astype(bf16).astype(f32)

    @pl.when(index > 0)
    def _():
        extended[0:RIM] = extended[BLOCK : BLOCK + RIM]

    values, lhs = scaled(piece)
    scale = row_scale(squares, values)
    gate[...] = ((acc[0] + dot(lhs, gate_x[0])) * scale).astype(bf16)
    x_raw = ((acc[1] + dot(lhs, gate_x[1])) * scale).astype(bf16)
    others_raw = ((acc_others[...] + dot(lhs, others[...])) * scale).astype(bf16)
    extended[RIM : RIM + BLOCK, :inner] = x_raw.astype(f32)
    extended[RIM : RIM + BLOCK, inner:] = others_raw[:, : 2 * STATE].astype(f32)
    step = jax.nn.softplus(others_raw[:, 2 * STATE :].astype(f32) + dt_bias[...])
    summed = taps[CONV : CONV + 1]
    for k in range(CONV):
        first = RIM - CONV + 1 + k
        summed = summed + taps[k : k + 1] * extended[first : first + BLOCK]
    conv = silu(summed)
    x_conv = conv[:, :inner].astype(bf16)
    bc = conv[:, inner:].astype(bf16)
    x_out[...] = x_conv
    bc_out[...] = bc
    x_wide = x_conv.astype(f32)
    by_step = dot(split(step), spread[...])
    by_end = dot(split(step * to_end[...]), spread[...])
    xs_out[...] = (x_wide * by_step).astype(bf16)
    weighted = (x_wide * by_end).astype(bf16)
    entering[0] = state[...]
    state[...] = keep[0] * state[...] + lax.dot_general(
        bc[:, :STATE], weighted, (((0,), (0,)), ((), ())), preferred_element_type=f32
    )

    @pl.when(index == pl.num_programs(0) - 1)
    def _():
        if last:
            half = STATE // 2
            chunks = inner // LANES
            joined = join[0] * state[...] + later[...]
            slabs[...] = jnp.zeros_like(slabs)
            for c in range(chunks):
                slabs[:, c] = joined[0:half, c * LANES : (c + 1) * LANES]
                slabs[:, chunks + c] = joined[half:STATE, c * LANES : (c + 1) * LANES]
            slabs[:, 2 * chunks] = jnp.broadcast_to(total[...], (half, LANES))
            payload[...] = slabs[...].astype(bf16)
        else:
            tail[...] = extended[BLOCK : BLOCK + RIM].astype(bf16)


def front(
    last, half, owner, acc, acc_others, piece, squares, gains, gate_x, others, near, taps, dt_bias, to_end,
    spread, keep, total, *more,
):
    width = piece.shape[1]
    inner = gate_x.shape[2]
    grid = to_end.shape[0] // BLOCK // 2
    rows = grid * BLOCK
    base = half * grid
    wide = inner + 2 * STATE
    pieces = STATE // 2

    def row(width, offset=0):
        return pl.BlockSpec((BLOCK, width), lambda i, o: (i + offset, 0))

    def whole(*shape):
        return pl.BlockSpec(shape, lambda i, o: (0,) * len(shape))

    def rim(width):
        return pl.BlockSpec((RIM, width), lambda i, o: (rows // RIM, 0))

    if last:
        operands = more
        extra = [whole(STATE, inner), pl.BlockSpec((1, 1, inner), lambda i, o: (9, 0, 0))]
        out_spec, out_shape = whole(pieces, 16, LANES), (pieces, 16, LANES)
        scratch = [pltpu.VMEM((pieces, 16, LANES), f32)]
    else:
        operands = (acc, acc_others, piece, squares)
        extra = [
            pl.BlockSpec((2, RIM, inner), lambda i, o: (0, rows // RIM, 0)),
            rim(acc_others.shape[1]), rim(width), rim(1),
        ]
        out_spec, out_shape = whole(RIM, wide), (RIM, wide)
        scratch = []
    return pl.pallas_call(
        functools.partial(front_kernel, inner, last),
        grid_spec=pltpu.PrefetchScalarGridSpec(
            num_scalar_prefetch=1,
            grid=(grid,),
            in_specs=[
                pl.BlockSpec((2, BLOCK, inner), lambda i, o: (0, i, 0)), row(acc_others.shape[1]),
                row(width), row(1),
                pl.BlockSpec((1, 1, width), lambda i, o: (o[0], 0, 0)),
                pl.BlockSpec((2, width, inner), lambda i, o: (0, o[0], 0)),
                pl.BlockSpec((width, others.shape[1]), lambda i, o: (o[0], 0)),
                whole(RIM, wide), whole(CONV + 1, wide),
                whole(1, LANES), row(LANES, base), whole(2 * LANES, inner),
                pl.BlockSpec((1, 1, inner), lambda i, o: (i + base, 0, 0)), whole(1, LANES),
            ] + extra,
            out_specs=[
                row(inner), row(inner), row(2 * STATE), row(inner),
                pl.BlockSpec((1, STATE, inner), lambda i, o: (i, 0, 0)),
                whole(STATE, inner), out_spec,
            ],
            scratch_shapes=[pltpu.VMEM((BLOCK + RIM, wide), f32)] + scratch,
        ),
        out_shape=[
            far_memory((rows, inner), bf16),
            far_memory((rows, inner), bf16),
            far_memory((rows, 2 * STATE), bf16),
            far_memory((rows, inner), bf16),
            far_memory((grid, STATE, inner), f32),
            jax.ShapeDtypeStruct((STATE, inner), f32),
            jax.ShapeDtypeStruct(out_shape, bf16),
        ],
        compiler_params=pltpu.CompilerParams(vmem_limit_bytes=VMEM),
        cost_estimate=LIGHT,
        name="front",
    )(owner, acc, acc_others, piece, squares, gains, gate_x, others, near, taps, dt_bias, to_end, spread, keep, total, *operands)


def scan_kernel(chunks, taken, spread, given, decays, sums):
    count = taken.shape[0]
    wide = taken[...].astype(f32)
    decays[...] = wide
    rows = decays[:, 2 * chunks]
    gains = jnp.exp(jnp.dot(rows.astype(bf16), spread[...], preferred_element_type=f32))
    sums[...] = wide
    decays[...] = jnp.zeros_like(decays)
    for c in range(chunks):
        part = gains[:, c * LANES : (c + 1) * LANES]
        decays[:, c] = part
        decays[:, chunks + c] = part
    running = jnp.zeros(taken.shape[1:], f32)
    for j in range(count):
        following = decays[j] * running + sums[j]
        sums[j] = running
        running = following
    given[...] = sums[...].astype(bf16)


def scan(taken, spread):
    chunks = spread.shape[1] // LANES
    return pl.pallas_call(
        functools.partial(scan_kernel, chunks),
        out_shape=jax.ShapeDtypeStruct(taken.shape, bf16),
        scratch_shapes=[pltpu.VMEM(taken.shape, f32), pltpu.VMEM(taken.shape, f32)],
        name="scan",
    )(taken, spread)


def inside_kernel(heads, bc, xs, decay, decay_t, out):
    both = bc[...]
    scores = lax.dot_general(
        both[:, STATE:], both[:, :STATE], (((1,), (1,)), ((), ())), preferred_element_type=f32
    )
    row = lax.broadcasted_iota(jnp.int32, (BLOCK, BLOCK), 0)
    column = lax.broadcasted_iota(jnp.int32, (BLOCK, BLOCK), 1)
    scores = jnp.where(row >= column, scores, 0.0)
    sums = decay[...]
    first = lax.broadcasted_iota(jnp.int32, (BLOCK, LANES), 1) < HEADDIM
    for pair in range(heads // 2):
        span = slice(pair * LANES, (pair + 1) * LANES)
        found = []
        for h in (2 * pair, 2 * pair + 1):
            gap = jnp.minimum(sums[:, h : h + 1] - decay_t[h : h + 1, :], 0.0)
            mix = (scores * jnp.exp(gap)).astype(bf16)
            found.append(jnp.dot(mix, xs[:, span], preferred_element_type=f32))
        out[:, span] = jnp.where(first, found[0], found[1])


def inside(bc, xs, decay, decay_t, half):
    rows, inner = xs.shape
    grid = rows // BLOCK
    base = half * grid
    return pl.pallas_call(
        functools.partial(inside_kernel, inner // HEADDIM),
        grid=(grid,),
        in_specs=[
            pl.BlockSpec((BLOCK, 2 * STATE), lambda i: (i, 0)),
            pl.BlockSpec((BLOCK, inner), lambda i: (i, 0)),
            pl.BlockSpec((BLOCK, LANES), lambda i: (i + base, 0)),
            pl.BlockSpec((16, BLOCK), lambda i: (0, i + base)),
        ],
        out_specs=pl.BlockSpec((BLOCK, inner), lambda i: (i, 0)),
        out_shape=far_memory((rows, inner), f32),
        compiler_params=pltpu.CompilerParams(vmem_limit_bytes=VMEM),
        cost_estimate=LIGHT,
        name="inside",
    )(bc, xs, decay, decay_t)


def tail_kernel(
    inner, half_index,
    y_in, x_conv, gate, bc, entering, taken, earlier, fade_in, before, skip, decay, spread, gain, weight,
    far, right, left, own, squares, slabs, incoming,
):
    chunks = inner // LANES

    @pl.when(pl.program_id(0) == 0)
    def _():
        squares[...] = jnp.zeros_like(squares)
        slabs[...] = taken[...].astype(f32)
        half = STATE // 2
        for c in range(chunks):
            incoming[0:half, c * LANES : (c + 1) * LANES] = slabs[:, c]
            incoming[half:STATE, c * LANES : (c + 1) * LANES] = slabs[:, chunks + c]
        if half_index:
            incoming[...] = earlier[...] + fade_in[0] * incoming[...]

    carried = (entering[0] + before[0] * incoming[...]).astype(bf16)
    fade = jnp.dot(split(jnp.exp(decay[...])), spread[...], preferred_element_type=f32)
    y = y_in[...] + fade * jnp.dot(bc[:, STATE:], carried, preferred_element_type=f32)
    y = y + skip[0] * x_conv[...].astype(f32)
    gated = y * silu(gate[...].astype(f32))
    step = pl.program_id(0)
    square = jnp.sum(gated * gated, axis=1, keepdims=True)
    squares[pl.ds(step, 1)] = jnp.transpose(jnp.broadcast_to(square, (BLOCK, LANES)))[:1]
    scaled = (gated * gain[...]).astype(bf16)
    width = far.shape[1]
    place = pl.ds(pl.multiple_of(step * BLOCK, BLOCK), BLOCK)
    outs = (own, right, far, left)
    for n, out in enumerate(outs):
        out[place] = jnp.dot(
            scaled, weight[:, n * width : (n + 1) * width], preferred_element_type=f32
        ).astype(bf16)

    @pl.when(step == pl.num_programs(0) - 1)
    def _():
        rows = far.shape[0] - 16
        parts = coded(squares[...])
        for out in outs:
            out[rows : rows + 16, :BLOCK] = parts
            out[rows : rows + 16, BLOCK:] = jnp.zeros((16, width - BLOCK), bf16)


def tail(half, y_in, x_conv, gate, bc, entering, taken, earlier, channels, decay, spread, gain, weight):
    rows, inner = y_in.shape
    grid = rows // BLOCK
    base = half * grid
    blocks = 2 * grid

    def channel(first, stride=0):
        return pl.BlockSpec((1, 1, inner), lambda i: (first + stride * i, 0, 0))

    width = weight.shape[1] // 4

    def row(width, offset=0):
        return pl.BlockSpec((BLOCK, width), lambda i: (i + offset, 0))

    def whole(*shape):
        return pl.BlockSpec(shape, lambda i: (0,) * len(shape))

    return pl.pallas_call(
        functools.partial(tail_kernel, inner, half),
        grid=(grid,),
        in_specs=[
            row(inner), row(inner), row(inner), row(2 * STATE),
            pl.BlockSpec((1, STATE, inner), lambda i: (i, 0, 0)),
            whole(*taken.shape), whole(STATE, inner), channel(2 * blocks), channel(blocks + base, 1),
            channel(2 * blocks + 2), row(LANES, base), whole(2 * LANES, inner), whole(1, inner),
            whole(*weight.shape),
        ],
        out_specs=[whole(rows + 16, width)] * 4,
        out_shape=[far_memory((rows + 16, width), bf16)] * 4,
        scratch_shapes=[
            pltpu.VMEM((8, BLOCK), f32), pltpu.VMEM(taken.shape, f32), pltpu.VMEM((STATE, inner), f32),
        ],
        compiler_params=pltpu.CompilerParams(vmem_limit_bytes=VMEM),
        cost_estimate=LIGHT,
        name="tail",
    )(
        y_in, x_conv, gate, bc, entering, taken, earlier, channels, channels, channels, decay, spread, gain,
        weight,
    )


def add_kernel(u, v, out):
    rows = out.shape[0] - 16
    out[:rows] = (u[:rows].astype(f32) + v[:rows].astype(f32)).astype(bf16)
    out[rows:] = coded(decoded(u[rows:]) + decoded(v[rows:]))


def add(u, v):
    return pl.pallas_call(
        add_kernel, out_shape=jax.ShapeDtypeStruct(u.shape, bf16), cost_estimate=LIGHT, name="add"
    )(u, v)


def finish_kernel(own_a, direct_a, arrived_a, own_b, direct_b, arrived_b, out):
    rows = own_a.shape[0] - 16
    for h, parts in enumerate(((own_a, direct_a, arrived_a), (own_b, direct_b, arrived_b))):
        squares = sum(decoded(p[rows:, :BLOCK]) for p in parts)
        scales = jnp.transpose(lax.rsqrt(squares * (1.0 / INNER) + eps))
        for k in range(rows // BLOCK):
            span = slice(k * BLOCK, (k + 1) * BLOCK)
            total = sum(p[span].astype(f32) for p in parts)
            first = h * rows + k * BLOCK
            out[first : first + BLOCK] = (total * scales[:, k : k + 1]).astype(bf16)


def finish(*parts):
    rows, width = parts[0].shape
    return pl.pallas_call(
        finish_kernel, out_shape=jax.ShapeDtypeStruct((2 * (rows - 16), width), bf16),
        cost_estimate=LIGHT, name="finish",
    )(*parts)


def per_device(
    hidden, norm_gain, zx_weight, bc_weight, dt_weight, conv_x, conv_bc, dt_bias,
    log_decay, skip_gain, out_gain, out_weight,
):
    rows, width = hidden.shape
    heads = dt_weight.shape[1]
    inner = zx_weight.shape[2]
    blocks = rows // BLOCK
    middle = rows // 2
    groups = lax.axis_size("head")
    places = lax.axis_size("ctx")
    me = lax.axis_index("head")
    to_right = [(i, (i + 1) % groups) for i in range(groups)]
    to_left = [(i, (i - 1) % groups) for i in range(groups)]

    def right(v):
        return lax.ppermute(v, "head", to_right)

    def left(v):
        return lax.ppermute(v, "head", to_left)

    bottom = jnp.concatenate([hidden[middle:], hidden[middle - RIM : middle]], axis=0)
    right_bottom, left_bottom = right(bottom), left(bottom)
    gate_x = jnp.transpose(zx_weight, (1, 0, 2))
    gains = norm_gain.reshape(groups, 1, width)
    owners = jnp.stack([me, lax.rem(me + groups - 1, groups), lax.rem(me + 1, groups)]).astype(jnp.int32)
    owner = lax.rem(me + 2, groups).astype(jnp.int32)[None]
    right_bottom, hidden, gate_x, log_decay, dt_weight, bc_weight = lax.optimization_barrier(
        (right_bottom, hidden, gate_x, log_decay, dt_weight, bc_weight)
    )
    decay, decay_t, to_end, channels, total, spread, thrice, others, taps, bias = prepare(
        jnp.transpose(log_decay), jnp.transpose(dt_weight), bc_weight, conv_x, conv_bc,
        dt_bias[None], skip_gain[None],
    )
    gate_x, = kept(gate_x)
    far_bottom = right(right_bottom)
    top = hidden[:middle]
    left_top = left(top)
    acc_b, others_b, squares_b = gather(owners, bottom, right_bottom, left_bottom, gains, gate_x, others)
    left_top, acc_b, top = lax.optimization_barrier((left_top, acc_b, top))
    far_top = left(left_top)
    right_top = right(top)

    channels = channels[:, None]
    gain = out_gain[None]

    no_rim = jnp.zeros((RIM, inner + 2 * STATE), bf16)
    gate_b, x_b, bc_b, xs_b, enter_b, state_b, raw_tail = front(
        False, 1, owner, *kept(acc_b, others_b), far_bottom, *kept(squares_b), gains, gate_x, others, no_rim, taps,
        bias, to_end, spread, channels, total,
    )
    near = lax.ppermute(raw_tail, "ctx", [(i, i + 1) for i in range(places - 1)])
    acc_a, others_a, squares_a = gather(owners, top, right_top, left_top, gains, gate_x, others)
    gate_a, x_a, bc_a, xs_a, enter_a, state_a, payload = front(
        True, 0, owner, *kept(acc_a, others_a), far_top, *kept(squares_a), gains, gate_x, others, near, taps, bias,
        to_end, spread, channels, total, state_b, channels,
    )
    taken = lax.all_to_all(payload, "ctx", 0, 0)
    inside_a = inside(*kept(bc_a, xs_a), decay, decay_t, 0)
    turned = jnp.concatenate(
        [
            lax.dynamic_slice_in_dim(out_weight, lax.rem(me + k, groups) * width, width, 1)
            for k in range(groups)
        ],
        axis=1,
    )
    taken, inside_a, turned = lax.optimization_barrier((taken, inside_a, turned))
    incoming = lax.all_to_all(scan(taken, thrice), "ctx", 0, 0)
    inside_b = inside(*kept(bc_b, xs_b), decay, decay_t, 1)
    incoming, inside_b = lax.optimization_barrier((incoming, inside_b))

    far_a, right_a, left_a, own_a = tail(
        0, *kept(inside_a, x_a, gate_a, bc_a, enter_a), incoming, state_a, channels, decay, spread,
        gain, turned,
    )
    passed_a, direct_a = right(far_a), left(left_a)
    far_b, right_b, left_b, own_b = tail(
        1, *kept(inside_b, x_b, gate_b, bc_b, enter_b), incoming, *kept(state_a), channels, decay,
        spread, gain, turned,
    )
    passed_b, direct_b = left(far_b), right(right_b)
    arrived_a = right(add(right_a, passed_a))
    arrived_b = left(add(left_b, passed_b))
    return finish(own_a, direct_a, arrived_a, own_b, direct_b, arrived_b)


def solution(mesh):
    placed = (
        P("ctx", "head"), P(), P(None, None, "head"), P(), P(None, "head"), P(None, "head"), P(),
        P("head"), P("ctx", "head"), P("head"), P("head"), P("head", None),
    )
    return jax.shard_map(
        per_device, mesh=mesh, in_specs=placed, out_specs=P("ctx", "head"), check_vma=False
    )
```

```python
import functools
import jax
import jax.numpy as jnp
from jax import lax
from jax.experimental import pallas as pl
from jax.experimental.pallas import tpu as pltpu
from jax.sharding import PartitionSpec as P

HEADDIM = 64
STATE = 128
CONV = 4
BLOCK = 256
INNER = 3072
D = 1536
LANES = 128
RIM = 16
VMEM = 24 * 2**20
LIGHT = pl.CostEstimate(flops=1024, bytes_accessed=1024, transcendentals=0)
eps = 1e-05
f32 = jnp.float32
bf16 = jnp.bfloat16


def kept(*arrays):
    return [pltpu.with_memory_space_constraint(v, pltpu.HBM) for v in arrays]


def far_memory(shape, kind):
    return pltpu.HBM(shape, kind)


def split(v):
    hi = v.astype(bf16)
    return jnp.concatenate([hi, (v - hi.astype(f32)).astype(bf16)], axis=1)


def coded(v):
    hi = v.astype(bf16).astype(f32)
    return jnp.concatenate([hi, v - hi], axis=0).astype(bf16)


def decoded(v):
    wide = v.astype(f32)
    return wide[:8] + wide[8:]


def silu(v):
    return 0.5 * v * (1.0 + jnp.tanh(0.5 * v))


def prepare_kernel(
    heads, inner, blocks,
    log_decay_t, dt_t, bc_weight, conv_x, conv_bc, dt_bias, skip_gain,
    decay, decay_t, to_end, channels, total, spread, thrice, others, taps, bias,
):
    lower = lax.broadcasted_iota(jnp.int32, (BLOCK, BLOCK), 0)
    upper = lax.broadcasted_iota(jnp.int32, (BLOCK, BLOCK), 1)
    ones = (lower <= upper).astype(f32)
    highest = lax.Precision.HIGHEST

    def dot(u, v):
        return jnp.dot(u, v, preferred_element_type=f32, precision=highest)

    def tall(v):
        padded = jnp.concatenate([v, jnp.zeros((LANES - heads, v.shape[1]), f32)], axis=0)
        return jnp.transpose(padded)

    lanes = lax.broadcasted_iota(jnp.int32, (LANES, inner), 0)
    head_of = lax.broadcasted_iota(jnp.int32, (LANES, inner), 1) // HEADDIM
    one_hot = (lanes == head_of).astype(f32)
    spread[0:LANES] = one_hot.astype(bf16)
    spread[LANES:] = one_hot.astype(bf16)
    three = (lanes == head_of) | (lanes == head_of + heads) | (lanes == head_of + 2 * heads)
    thrice[...] = three.astype(f32).astype(bf16)
    decay_t[...] = jnp.zeros_like(decay_t)
    totals = []
    for k in range(blocks):
        span = slice(k * BLOCK, (k + 1) * BLOCK)
        sums_t = dot(log_decay_t[:, span], ones)
        decay_t[0:heads, span] = sums_t
        sums = tall(sums_t)
        decay[span] = sums
        last = sums[BLOCK - 1 : BLOCK]
        to_end[span] = jnp.exp(last - sums)
        totals.append(last)
    rows = [jnp.exp(v) for v in totals]
    fades = []
    for h in range(2):
        passed = jnp.zeros((1, LANES), f32)
        for k in range(blocks // 2):
            rows.append(jnp.exp(passed))
            passed = passed + totals[h * (blocks // 2) + k]
        fades.append(passed)
    rows += [jnp.exp(v) for v in fades]

    def row(v):
        return jnp.concatenate([v, jnp.zeros((1, LANES - heads), f32)], axis=1)

    rows.append(row(skip_gain[...]))
    rows.append(jnp.ones((1, LANES), f32))
    while len(rows) < 16:
        rows.append(jnp.zeros((1, LANES), f32))
    channels[...] = dot(jnp.concatenate(rows, axis=0), one_hot)
    whole = fades[0] + fades[1]
    high = whole.astype(bf16).astype(f32)
    mid = (whole - high).astype(bf16).astype(f32)
    low = whole - high - mid
    total[...] = jnp.concatenate(
        [high[:, :heads], mid[:, :heads], low[:, :heads], jnp.zeros((1, LANES - 3 * heads), f32)], axis=1
    )
    bias[...] = row(dt_bias[...])
    others[:, : 2 * STATE] = bc_weight[...]
    others[:, 2 * STATE :] = tall(dt_t[...].astype(f32)).astype(bf16)
    taps[0 : CONV + 1, :inner] = conv_x[...]
    taps[0 : CONV + 1, inner:] = conv_bc[...]


def prepare(log_decay_t, dt_t, bc_weight, conv_x, conv_bc, dt_bias, skip_gain):
    heads, rows = log_decay_t.shape
    inner = conv_x.shape[1]
    blocks = rows // BLOCK
    shapes = [
        ((rows, LANES), f32), ((16, rows), f32), ((rows, LANES), f32), ((16, inner), f32),
        ((1, LANES), f32), ((2 * LANES, inner), bf16), ((LANES, inner), bf16),
        ((D, 2 * STATE + LANES), bf16), ((CONV + 1, inner + 2 * STATE), f32), ((1, LANES), f32),
    ]
    return pl.pallas_call(
        functools.partial(prepare_kernel, heads, inner, blocks),
        out_shape=[
            (jax.ShapeDtypeStruct if k == 3 else far_memory)(*v) for k, v in enumerate(shapes)
        ],
        compiler_params=pltpu.CompilerParams(vmem_limit_bytes=VMEM),
        cost_estimate=LIGHT,
        name="prepare",
    )(log_decay_t, dt_t, bc_weight, conv_x, conv_bc, dt_bias, skip_gain)


def gather_kernel(
    owners, own, from_left, from_right, gain_0, gain_1, gain_2, w_0, w_1, w_2, o_0, o_1, o_2,
    acc, acc_others, squares, lhs,
):
    width = own.shape[1]
    square = None
    for k, (piece, gain) in enumerate(((own, gain_0), (from_left, gain_1), (from_right, gain_2))):
        values = piece[...].astype(f32)
        lhs[:, k * width : (k + 1) * width] = (values * gain[0]).astype(bf16)
        part = jnp.sum(values * values, axis=1, keepdims=True)
        square = part if square is None else square + part
    squares[...] = square
    acc[...] = jnp.dot(
        lhs[...], jnp.concatenate([w_0[0], w_1[0], w_2[0]], axis=0), preferred_element_type=f32
    )
    acc_others[...] = jnp.dot(
        lhs[...], jnp.concatenate([o_0[...], o_1[...], o_2[...]], axis=0), preferred_element_type=f32
    )


def gather(owners, own, from_left, from_right, gains, gate_x, others):
    rows, width = own.shape
    inner = gate_x.shape[2]
    narrow = others.shape[1]

    def whole(*shape):
        return pl.BlockSpec(shape, lambda n, o: (0,) * len(shape))

    def gain(k):
        return pl.BlockSpec((1, 1, width), lambda n, o: (o[k], 0, 0))

    def wide(k):
        return pl.BlockSpec((1, width, inner), lambda n, o: (1, o[k], 0))

    def small(k):
        return pl.BlockSpec((width, narrow), lambda n, o: (o[k], 0))

    return pl.pallas_call(
        gather_kernel,
        grid_spec=pltpu.PrefetchScalarGridSpec(
            num_scalar_prefetch=1,
            grid=(1,),
            in_specs=[whole(rows, width)] * 3 + [f(k) for f in (gain, wide, small) for k in range(3)],
            out_specs=[
                whole(rows, inner), whole(rows, narrow), whole(rows, 1),
            ],
            scratch_shapes=[pltpu.VMEM((rows, 3 * width), bf16)],
        ),
        out_shape=[
            far_memory((rows, inner), f32), far_memory((rows, narrow), f32), far_memory((rows, 1), f32),
        ],
        compiler_params=pltpu.CompilerParams(vmem_limit_bytes=VMEM),
        cost_estimate=LIGHT,
        name="gather",
    )(owners, own, from_left, from_right, gains, gains, gains, gate_x, gate_x, gate_x, others, others, others)


def gate_kernel(
    owners, own, from_left, from_right, far, gain_0, gain_1, gain_2, gain_3, w_0, w_1, w_2, w_3,
    squares, out, lhs,
):
    width = own.shape[1]
    for k, (piece, gain) in enumerate(
        ((own, gain_0), (from_left, gain_1), (from_right, gain_2), (far, gain_3))
    ):
        values = piece[...].astype(f32)
        lhs[:, k * width : (k + 1) * width] = (values * gain[0]).astype(bf16)
    square = squares[...] + jnp.sum(values * values, axis=1, keepdims=True)
    full = jnp.dot(
        lhs[...], jnp.concatenate([w_0[0], w_1[0], w_2[0], w_3[0]], axis=0), preferred_element_type=f32
    )
    out[...] = (full * lax.rsqrt(square * (1.0 / D) + eps)).astype(bf16)


def project_gate(rows, owners, pieces, gains, gate_x, squares):
    width = pieces[0].shape[1]
    inner = gate_x.shape[2]
    grid = rows // BLOCK

    def row(width):
        return pl.BlockSpec((BLOCK, width), lambda i, o: (i, 0))

    def gain(k):
        return pl.BlockSpec((1, 1, width), lambda i, o: (o[k], 0, 0))

    def wide(k):
        return pl.BlockSpec((1, width, inner), lambda i, o: (0, o[k], 0))

    return pl.pallas_call(
        gate_kernel,
        grid_spec=pltpu.PrefetchScalarGridSpec(
            num_scalar_prefetch=1,
            grid=(grid,),
            in_specs=[row(width)] * 4 + [f(k) for f in (gain, wide) for k in range(4)] + [row(1)],
            out_specs=row(inner),
            scratch_shapes=[pltpu.VMEM((BLOCK, 4 * width), bf16)],
        ),
        out_shape=far_memory((rows, inner), bf16),
        compiler_params=pltpu.CompilerParams(vmem_limit_bytes=VMEM),
        cost_estimate=LIGHT,
        name="gate",
    )(owners, *pieces, *[gains] * 4, *[gate_x] * 4, squares)


def front_kernel(
    inner, last,
    owner, acc, acc_others, piece, squares, gain, gate_x, others, near, taps, dt_bias, to_end, spread, keep, total,
    *rest,
):
    if last:
        later, join, x_out, bc_out, xs_out, entering, state, payload, extended, slabs = rest
    else:
        rim_acc, rim_others, rim_piece, rim_squares, x_out, bc_out, xs_out, entering, state, tail, extended = rest
    index = pl.program_id(0)
    wide = inner + 2 * STATE

    def scaled(piece):
        values = piece[...].astype(f32)
        return values, (values * gain[0]).astype(bf16)

    def row_scale(squares, values):
        square = squares[...] + jnp.sum(values * values, axis=1, keepdims=True)
        return lax.rsqrt(square * (1.0 / D) + eps)

    def dot(u, v):
        return jnp.dot(u, v, preferred_element_type=f32)

    @pl.when(index == 0)
    def _():
        state[...] = jnp.zeros_like(state)
        if last:
            extended[0:RIM] = near[...].astype(f32)
        else:
            values, lhs = scaled(rim_piece)
            scale = row_scale(rim_squares, values)
            x_rim = (rim_acc[...] + dot(lhs, gate_x[0])) * scale
            bc_rim = (
                rim_others[:, : 2 * STATE] + dot(lhs, others[:, : 2 * STATE])
            ) * scale
            extended[0:RIM, :inner] = x_rim.astype(bf16).astype(f32)
            extended[0:RIM, inner:] = bc_rim.astype(bf16).astype(f32)

    @pl.when(index > 0)
    def _():
        extended[0:RIM] = extended[BLOCK : BLOCK + RIM]

    values, lhs = scaled(piece)
    scale = row_scale(squares, values)
    x_raw = ((acc[...] + dot(lhs, gate_x[0])) * scale).astype(bf16)
    others_raw = ((acc_others[...] + dot(lhs, others[...])) * scale).astype(bf16)
    extended[RIM : RIM + BLOCK, :inner] = x_raw.astype(f32)
    extended[RIM : RIM + BLOCK, inner:] = others_raw[:, : 2 * STATE].astype(f32)
    step = jax.nn.softplus(others_raw[:, 2 * STATE :].astype(f32) + dt_bias[...])
    summed = taps[CONV : CONV + 1]
    for k in range(CONV):
        first = RIM - CONV + 1 + k
        summed = summed + taps[k : k + 1] * extended[first : first + BLOCK]
    conv = silu(summed)
    x_conv = conv[:, :inner].astype(bf16)
    bc = conv[:, inner:].astype(bf16)
    x_out[...] = x_conv
    bc_out[...] = bc
    x_wide = x_conv.astype(f32)
    by_step = dot(split(step), spread[...])
    by_end = dot(split(step * to_end[...]), spread[...])
    xs_out[...] = (x_wide * by_step).astype(bf16)
    weighted = (x_wide * by_end).astype(bf16)
    entering[0] = state[...]
    state[...] = keep[0] * state[...] + lax.dot_general(
        bc[:, :STATE], weighted, (((0,), (0,)), ((), ())), preferred_element_type=f32
    )

    @pl.when(index == pl.num_programs(0) - 1)
    def _():
        if last:
            half = STATE // 2
            chunks = inner // LANES
            joined = join[0] * state[...] + later[...]
            slabs[...] = jnp.zeros_like(slabs)
            for c in range(chunks):
                slabs[:, c] = joined[0:half, c * LANES : (c + 1) * LANES]
                slabs[:, chunks + c] = joined[half:STATE, c * LANES : (c + 1) * LANES]
            slabs[:, 2 * chunks] = jnp.broadcast_to(total[...], (half, LANES))
            payload[...] = slabs[...].astype(bf16)
        else:
            tail[...] = extended[BLOCK : BLOCK + RIM].astype(bf16)


def front(
    last, half, owner, acc, acc_others, piece, squares, gains, gate_x, others, near, taps, dt_bias, to_end,
    spread, keep, total, *more,
):
    width = piece.shape[1]
    inner = gate_x.shape[2]
    grid = to_end.shape[0] // BLOCK // 2
    rows = grid * BLOCK
    base = half * grid
    wide = inner + 2 * STATE
    pieces = STATE // 2

    def row(width, offset=0):
        return pl.BlockSpec((BLOCK, width), lambda i, o: (i + offset, 0))

    def whole(*shape):
        return pl.BlockSpec(shape, lambda i, o: (0,) * len(shape))

    def rim(width):
        return pl.BlockSpec((RIM, width), lambda i, o: (rows // RIM, 0))

    if last:
        operands = more
        extra = [whole(STATE, inner), pl.BlockSpec((1, 1, inner), lambda i, o: (9, 0, 0))]
        out_spec, out_shape = whole(pieces, 16, LANES), (pieces, 16, LANES)
        scratch = [pltpu.VMEM((pieces, 16, LANES), f32)]
    else:
        operands = (acc, acc_others, piece, squares)
        extra = [
            rim(inner), rim(acc_others.shape[1]), rim(width), rim(1),
        ]
        out_spec, out_shape = whole(RIM, wide), (RIM, wide)
        scratch = []
    return pl.pallas_call(
        functools.partial(front_kernel, inner, last),
        grid_spec=pltpu.PrefetchScalarGridSpec(
            num_scalar_prefetch=1,
            grid=(grid,),
            in_specs=[
                row(inner), row(acc_others.shape[1]),
                row(width), row(1),
                pl.BlockSpec((1, 1, width), lambda i, o: (o[0], 0, 0)),
                pl.BlockSpec((1, width, inner), lambda i, o: (1, o[0], 0)),
                pl.BlockSpec((width, others.shape[1]), lambda i, o: (o[0], 0)),
                whole(RIM, wide), whole(CONV + 1, wide),
                whole(1, LANES), row(LANES, base), whole(2 * LANES, inner),
                pl.BlockSpec((1, 1, inner), lambda i, o: (i + base, 0, 0)), whole(1, LANES),
            ] + extra,
            out_specs=[
                row(inner), row(2 * STATE), row(inner),
                pl.BlockSpec((1, STATE, inner), lambda i, o: (i, 0, 0)),
                whole(STATE, inner), out_spec,
            ],
            scratch_shapes=[pltpu.VMEM((BLOCK + RIM, wide), f32)] + scratch,
        ),
        out_shape=[
            far_memory((rows, inner), bf16),
            far_memory((rows, 2 * STATE), bf16),
            far_memory((rows, inner), bf16),
            far_memory((grid, STATE, inner), f32),
            jax.ShapeDtypeStruct((STATE, inner), f32),
            jax.ShapeDtypeStruct(out_shape, bf16),
        ],
        compiler_params=pltpu.CompilerParams(vmem_limit_bytes=VMEM),
        cost_estimate=LIGHT,
        name="front",
    )(owner, acc, acc_others, piece, squares, gains, gate_x, others, near, taps, dt_bias, to_end, spread, keep, total, *operands)


def scan_kernel(chunks, taken, spread, given, decays, sums):
    count = taken.shape[0]
    wide = taken[...].astype(f32)
    decays[...] = wide
    rows = decays[:, 2 * chunks]
    gains = jnp.exp(jnp.dot(rows.astype(bf16), spread[...], preferred_element_type=f32))
    sums[...] = wide
    decays[...] = jnp.zeros_like(decays)
    for c in range(chunks):
        part = gains[:, c * LANES : (c + 1) * LANES]
        decays[:, c] = part
        decays[:, chunks + c] = part
    running = jnp.zeros(taken.shape[1:], f32)
    for j in range(count):
        following = decays[j] * running + sums[j]
        sums[j] = running
        running = following
    given[...] = sums[...].astype(bf16)


def scan(taken, spread):
    chunks = spread.shape[1] // LANES
    return pl.pallas_call(
        functools.partial(scan_kernel, chunks),
        out_shape=jax.ShapeDtypeStruct(taken.shape, bf16),
        scratch_shapes=[pltpu.VMEM(taken.shape, f32), pltpu.VMEM(taken.shape, f32)],
        compiler_params=pltpu.CompilerParams(vmem_limit_bytes=VMEM // 2),
        cost_estimate=LIGHT,
        name="scan",
    )(taken, spread)


def inside_kernel(heads, bc, xs, decay, decay_t, out):
    both = bc[...]
    scores = lax.dot_general(
        both[:, STATE:], both[:, :STATE], (((1,), (1,)), ((), ())), preferred_element_type=f32
    )
    row = lax.broadcasted_iota(jnp.int32, (BLOCK, BLOCK), 0)
    column = lax.broadcasted_iota(jnp.int32, (BLOCK, BLOCK), 1)
    scores = jnp.where(row >= column, scores, 0.0)
    sums = decay[...]
    first = lax.broadcasted_iota(jnp.int32, (BLOCK, LANES), 1) < HEADDIM
    for pair in range(heads // 2):
        span = slice(pair * LANES, (pair + 1) * LANES)
        found = []
        for h in (2 * pair, 2 * pair + 1):
            gap = jnp.minimum(sums[:, h : h + 1] - decay_t[h : h + 1, :], 0.0)
            mix = (scores * jnp.exp(gap)).astype(bf16)
            found.append(jnp.dot(mix, xs[:, span], preferred_element_type=f32))
        out[:, span] = jnp.where(first, found[0], found[1])


def inside(bc, xs, decay, decay_t, half):
    rows, inner = xs.shape
    grid = rows // BLOCK
    base = half * grid
    return pl.pallas_call(
        functools.partial(inside_kernel, inner // HEADDIM),
        grid=(grid,),
        in_specs=[
            pl.BlockSpec((BLOCK, 2 * STATE), lambda i: (i, 0)),
            pl.BlockSpec((BLOCK, inner), lambda i: (i, 0)),
            pl.BlockSpec((BLOCK, LANES), lambda i: (i + base, 0)),
            pl.BlockSpec((16, BLOCK), lambda i: (0, i + base)),
        ],
        out_specs=pl.BlockSpec((BLOCK, inner), lambda i: (i, 0)),
        out_shape=far_memory((rows, inner), f32),
        compiler_params=pltpu.CompilerParams(vmem_limit_bytes=VMEM),
        cost_estimate=LIGHT,
        name="inside",
    )(bc, xs, decay, decay_t)


def tail_kernel(
    inner, half_index,
    y_in, x_conv, gate, bc, entering, taken, earlier, fade_in, before, skip, decay, spread, gain, weight,
    far, scaled_out, squares, slabs, incoming,
):
    chunks = inner // LANES

    @pl.when(pl.program_id(0) == 0)
    def _():
        squares[...] = jnp.zeros_like(squares)
        slabs[...] = taken[...].astype(f32)
        half = STATE // 2
        for c in range(chunks):
            incoming[0:half, c * LANES : (c + 1) * LANES] = slabs[:, c]
            incoming[half:STATE, c * LANES : (c + 1) * LANES] = slabs[:, chunks + c]
        if half_index:
            incoming[...] = earlier[...] + fade_in[0] * incoming[...]

    carried = (entering[0] + before[0] * incoming[...]).astype(bf16)
    fade = jnp.dot(split(jnp.exp(decay[...])), spread[...], preferred_element_type=f32)
    y = y_in[...] + fade * jnp.dot(bc[:, STATE:], carried, preferred_element_type=f32)
    y = y + skip[0] * x_conv[...].astype(f32)
    gated = y * silu(gate[...].astype(f32))
    step = pl.program_id(0)
    square = jnp.sum(gated * gated, axis=1, keepdims=True)
    squares[pl.ds(step, 1)] = jnp.transpose(jnp.broadcast_to(square, (BLOCK, LANES)))[:1]
    scaled = (gated * gain[...]).astype(bf16)
    width = far.shape[1]
    place = pl.ds(pl.multiple_of(step * BLOCK, BLOCK), BLOCK)
    far[place] = jnp.dot(scaled, weight[...], preferred_element_type=f32).astype(bf16)
    scaled_out[place] = scaled

    @pl.when(step == pl.num_programs(0) - 1)
    def _():
        rows = far.shape[0] - 16
        parts = coded(squares[...])
        for out in (far, scaled_out):
            out[rows : rows + 16, :BLOCK] = parts
            out[rows : rows + 16, BLOCK:] = jnp.zeros((16, out.shape[1] - BLOCK), bf16)


def tail(half, y_in, x_conv, gate, bc, entering, taken, earlier, channels, decay, spread, gain, weight):
    rows, inner = y_in.shape
    grid = rows // BLOCK
    base = half * grid
    blocks = 2 * grid

    def channel(first, stride=0):
        return pl.BlockSpec((1, 1, inner), lambda i: (first + stride * i, 0, 0))

    width = weight.shape[1] // 4

    def row(width, offset=0):
        return pl.BlockSpec((BLOCK, width), lambda i: (i + offset, 0))

    def whole(*shape):
        return pl.BlockSpec(shape, lambda i: (0,) * len(shape))

    return pl.pallas_call(
        functools.partial(tail_kernel, inner, half),
        grid=(grid,),
        in_specs=[
            row(inner), row(inner), row(inner), row(2 * STATE),
            pl.BlockSpec((1, STATE, inner), lambda i: (i, 0, 0)),
            whole(*taken.shape), whole(STATE, inner), channel(2 * blocks), channel(blocks + base, 1),
            channel(2 * blocks + 2), row(LANES, base), whole(2 * LANES, inner), whole(1, inner),
            pl.BlockSpec((inner, width), lambda i: (0, 2)),
        ],
        out_specs=[whole(rows + 16, width), whole(rows + 16, inner)],
        out_shape=[far_memory((rows + 16, width), bf16), far_memory((rows + 16, inner), bf16)],
        scratch_shapes=[
            pltpu.VMEM((8, BLOCK), f32), pltpu.VMEM(taken.shape, f32), pltpu.VMEM((STATE, inner), f32),
        ],
        compiler_params=pltpu.CompilerParams(vmem_limit_bytes=VMEM),
        cost_estimate=pl.CostEstimate(
            flops=2 * rows * inner * (weight.shape[1] + STATE),
            bytes_accessed=rows * inner * 10 + weight.size * 2, transcendentals=rows * inner,
        ),
        name="tail",
    )(
        y_in, x_conv, gate, bc, entering, taken, earlier, channels, channels, channels, decay, spread, gain,
        weight,
    )


def rest_kernel(scaled_b, scaled_a, weight, right_b, left_b, own_b, left_a, right_a, own_a):
    width = own_a.shape[1]
    for scaled, outs in ((scaled_b, (own_b, right_b, left_b)), (scaled_a, (own_a, right_a, left_a))):
        rows = scaled.shape[0] - 16
        for n, out in zip((0, 1, 3), outs):
            out[:rows] = jnp.dot(
                scaled[:rows], weight[:, n * width : (n + 1) * width], preferred_element_type=f32
            ).astype(bf16)
            out[rows:] = scaled[rows:, :width]


def rest(scaled_b, scaled_a, weight):
    shape = jax.ShapeDtypeStruct((scaled_a.shape[0], weight.shape[1] // 4), bf16)
    return pl.pallas_call(
        rest_kernel,
        out_shape=[shape] * 6,
        compiler_params=pltpu.CompilerParams(vmem_limit_bytes=VMEM),
        cost_estimate=pl.CostEstimate(
            flops=3 * scaled_a.size * weight.shape[1], bytes_accessed=4 * scaled_a.size + 2 * weight.size,
            transcendentals=0,
        ),
        name="rest",
    )(scaled_b, scaled_a, weight)


def add_kernel(u, v, out):
    rows = out.shape[0] - 16
    out[:rows] = (u[:rows].astype(f32) + v[:rows].astype(f32)).astype(bf16)
    out[rows:] = coded(decoded(u[rows:]) + decoded(v[rows:]))


def add(u, v):
    return pl.pallas_call(
        add_kernel, out_shape=jax.ShapeDtypeStruct(u.shape, bf16), cost_estimate=LIGHT, name="add",
        compiler_params=pltpu.CompilerParams(vmem_limit_bytes=VMEM // 2),
    )(u, v)


def finish_kernel(own_a, direct_a, arrived_a, own_b, direct_b, arrived_b, out):
    rows = own_a.shape[0] - 16
    for h, parts in enumerate(((own_a, direct_a, arrived_a), (own_b, direct_b, arrived_b))):
        squares = sum(decoded(p[rows:, :BLOCK]) for p in parts)
        scales = jnp.transpose(lax.rsqrt(squares * (1.0 / INNER) + eps))
        for k in range(rows // BLOCK):
            span = slice(k * BLOCK, (k + 1) * BLOCK)
            total = sum(p[span].astype(f32) for p in parts)
            first = h * rows + k * BLOCK
            out[first : first + BLOCK] = (total * scales[:, k : k + 1]).astype(bf16)


def finish(*parts):
    rows, width = parts[0].shape
    return pl.pallas_call(
        finish_kernel, out_shape=jax.ShapeDtypeStruct((2 * (rows - 16), width), bf16),
        compiler_params=pltpu.CompilerParams(vmem_limit_bytes=VMEM // 2),
        cost_estimate=LIGHT, name="finish",
    )(*parts)


def per_device(
    hidden, norm_gain, zx_weight, bc_weight, dt_weight, conv_x, conv_bc, dt_bias,
    log_decay, skip_gain, out_gain, out_weight,
):
    rows, width = hidden.shape
    heads = dt_weight.shape[1]
    inner = zx_weight.shape[2]
    blocks = rows // BLOCK
    middle = rows // 2
    groups = lax.axis_size("head")
    places = lax.axis_size("ctx")
    me = lax.axis_index("head")
    to_right = [(i, (i + 1) % groups) for i in range(groups)]
    to_left = [(i, (i - 1) % groups) for i in range(groups)]

    def right(v):
        return lax.ppermute(v, "head", to_right)

    def left(v):
        return lax.ppermute(v, "head", to_left)

    bottom = jnp.concatenate([hidden[middle:], hidden[middle - RIM : middle]], axis=0)
    right_bottom, left_bottom = right(bottom), left(bottom)
    gate_x = jnp.transpose(zx_weight, (1, 0, 2))
    gains = norm_gain.reshape(groups, 1, width)
    owners = jnp.stack([me, lax.rem(me + groups - 1, groups), lax.rem(me + 1, groups)]).astype(jnp.int32)
    owner = lax.rem(me + 2, groups).astype(jnp.int32)[None]
    all_owners = jnp.concatenate([owners, owner])
    prepared = prepare(
        *kept(
            jnp.transpose(log_decay), jnp.transpose(dt_weight), bc_weight, conv_x, conv_bc,
            dt_bias[None], skip_gain[None],
        )
    )
    right_bottom, hidden, gate_x, prepared = lax.optimization_barrier(
        (right_bottom, hidden, gate_x, prepared)
    )
    decay, decay_t, to_end, channels, total, spread, thrice, others, taps, bias = prepared
    gate_x, = kept(gate_x)
    far_bottom = right(right_bottom)
    top = hidden[:middle]
    left_top = left(top)
    acc_b, others_b, squares_b = gather(owners, bottom, right_bottom, left_bottom, gains, gate_x, others)
    left_top, acc_b, top = lax.optimization_barrier((left_top, acc_b, top))
    far_top = left(left_top)
    right_top = right(top)

    channels = channels[:, None]
    gain = out_gain[None]

    no_rim = jnp.zeros((RIM, inner + 2 * STATE), bf16)
    x_b, bc_b, xs_b, enter_b, state_b, raw_tail = front(
        False, 1, owner, *kept(acc_b, others_b), far_bottom, *kept(squares_b), gains, gate_x, others, no_rim, taps,
        bias, to_end, spread, channels, total,
    )
    near = lax.ppermute(raw_tail, "ctx", [(i, i + 1) for i in range(places - 1)])
    acc_a, others_a, squares_a = gather(owners, top, right_top, left_top, gains, gate_x, others)
    x_a, bc_a, xs_a, enter_a, state_a, payload = front(
        True, 0, owner, *kept(acc_a, others_a), far_top, *kept(squares_a), gains, gate_x, others, near, taps, bias,
        to_end, spread, channels, total, state_b, channels,
    )
    taken = lax.all_to_all(payload, "ctx", 0, 0)
    inside_a = inside(*kept(bc_a, xs_a), decay, decay_t, 0)
    turned = jnp.concatenate(
        [
            lax.dynamic_slice_in_dim(out_weight, lax.rem(me + k, groups) * width, width, 1)
            for k in range(groups)
        ],
        axis=1,
    )
    gate_a = project_gate(
        middle, all_owners, kept(top, right_top, left_top, far_top), gains, gate_x, *kept(squares_a)
    )
    taken, inside_a, turned, gate_a = lax.optimization_barrier((taken, inside_a, turned, gate_a))
    incoming = lax.all_to_all(scan(taken, thrice), "ctx", 0, 0)
    inside_b = inside(*kept(bc_b, xs_b), decay, decay_t, 1)
    gate_b = project_gate(
        middle, all_owners, kept(bottom, right_bottom, left_bottom, far_bottom), gains, gate_x,
        *kept(squares_b),
    )
    incoming, inside_b, gate_b = lax.optimization_barrier((incoming, inside_b, gate_b))

    far_b, scaled_b = tail(
        1, *kept(inside_b, x_b, gate_b, bc_b, enter_b), incoming, *kept(state_a), channels, decay,
        spread, gain, turned,
    )
    far_a, scaled_a = tail(
        0, *kept(inside_a, x_a, gate_a, bc_a, enter_a), incoming, state_a, channels, decay, spread,
        gain, turned,
    )
    passed_b = left(far_b)
    passed_a = right(far_a)
    right_b, left_b, own_b, left_a, right_a, own_a = rest(scaled_b, scaled_a, turned)
    direct_a, direct_b = left(left_a), right(right_b)
    arrived_a = right(add(right_a, passed_a))
    arrived_b = left(add(left_b, passed_b))
    return finish(own_a, direct_a, arrived_a, own_b, direct_b, arrived_b)


def solution(mesh):
    placed = (
        P("ctx", "head"), P(), P(None, None, "head"), P(), P(None, "head"), P(None, "head"), P(),
        P("head"), P("ctx", "head"), P("head"), P("head"), P("head", None),
    )
    return jax.shard_map(
        per_device, mesh=mesh, in_specs=placed, out_specs=P("ctx", "head"), check_vma=False
    )
```

```python
import functools
import jax
import jax.numpy as jnp
from jax import lax
from jax.experimental import pallas as pl
from jax.experimental.pallas import tpu as pltpu
from jax.sharding import PartitionSpec as P

HEADDIM = 64
STATE = 128
CONV = 4
BLOCK = 256
INNER = 3072
D = 1536
LANES = 128
RIM = 16
VMEM = 24 * 2**20
LIGHT = pl.CostEstimate(flops=1024, bytes_accessed=1024, transcendentals=0)
eps = 1e-05
f32 = jnp.float32
bf16 = jnp.bfloat16


def kept(*arrays):
    return [pltpu.with_memory_space_constraint(v, pltpu.HBM) for v in arrays]


def far_memory(shape, kind):
    return pltpu.HBM(shape, kind)


def split(v):
    hi = v.astype(bf16)
    return jnp.concatenate([hi, (v - hi.astype(f32)).astype(bf16)], axis=1)


def coded(v):
    hi = v.astype(bf16).astype(f32)
    return jnp.concatenate([hi, v - hi], axis=0).astype(bf16)


def decoded(v):
    wide = v.astype(f32)
    return wide[:8] + wide[8:]


def silu(v):
    return 0.5 * v * (1.0 + jnp.tanh(0.5 * v))


def prepare_kernel(
    heads, inner, blocks,
    log_decay_t, dt_t, bc_weight, conv_x, conv_bc, dt_bias, skip_gain,
    decay, decay_t, to_end, channels, total, spread, thrice, others, taps, bias,
):
    lower = lax.broadcasted_iota(jnp.int32, (BLOCK, BLOCK), 0)
    upper = lax.broadcasted_iota(jnp.int32, (BLOCK, BLOCK), 1)
    ones = (lower <= upper).astype(f32)
    highest = lax.Precision.HIGHEST

    def dot(u, v):
        return jnp.dot(u, v, preferred_element_type=f32, precision=highest)

    def tall(v):
        padded = jnp.concatenate([v, jnp.zeros((LANES - heads, v.shape[1]), f32)], axis=0)
        return jnp.transpose(padded)

    lanes = lax.broadcasted_iota(jnp.int32, (LANES, inner), 0)
    head_of = lax.broadcasted_iota(jnp.int32, (LANES, inner), 1) // HEADDIM
    one_hot = (lanes == head_of).astype(f32)
    spread[0:LANES] = one_hot.astype(bf16)
    spread[LANES:] = one_hot.astype(bf16)
    three = (lanes == head_of) | (lanes == head_of + heads) | (lanes == head_of + 2 * heads)
    thrice[...] = three.astype(f32).astype(bf16)
    decay_t[...] = jnp.zeros_like(decay_t)
    totals = []
    for k in range(blocks):
        span = slice(k * BLOCK, (k + 1) * BLOCK)
        sums_t = dot(log_decay_t[:, span], ones)
        decay_t[0:heads, span] = sums_t
        sums = tall(sums_t)
        decay[span] = sums
        last = sums[BLOCK - 1 : BLOCK]
        to_end[span] = jnp.exp(last - sums)
        totals.append(last)
    rows = [jnp.exp(v) for v in totals]
    fades = []
    for h in range(2):
        passed = jnp.zeros((1, LANES), f32)
        for k in range(blocks // 2):
            rows.append(jnp.exp(passed))
            passed = passed + totals[h * (blocks // 2) + k]
        fades.append(passed)
    rows += [jnp.exp(v) for v in fades]

    def row(v):
        return jnp.concatenate([v, jnp.zeros((1, LANES - heads), f32)], axis=1)

    rows.append(row(skip_gain[...]))
    rows.append(jnp.ones((1, LANES), f32))
    while len(rows) < 16:
        rows.append(jnp.zeros((1, LANES), f32))
    channels[...] = dot(jnp.concatenate(rows, axis=0), one_hot)
    whole = fades[0] + fades[1]
    high = whole.astype(bf16).astype(f32)
    mid = (whole - high).astype(bf16).astype(f32)
    low = whole - high - mid
    total[...] = jnp.concatenate(
        [high[:, :heads], mid[:, :heads], low[:, :heads], jnp.zeros((1, LANES - 3 * heads), f32)], axis=1
    )
    bias[...] = row(dt_bias[...])
    others[:, : 2 * STATE] = bc_weight[...]
    others[:, 2 * STATE :] = tall(dt_t[...].astype(f32)).astype(bf16)
    taps[0 : CONV + 1, :inner] = conv_x[...]
    taps[0 : CONV + 1, inner:] = conv_bc[...]


def prepare(log_decay_t, dt_t, bc_weight, conv_x, conv_bc, dt_bias, skip_gain):
    heads, rows = log_decay_t.shape
    inner = conv_x.shape[1]
    blocks = rows // BLOCK
    shapes = [
        ((rows, LANES), f32), ((16, rows), f32), ((rows, LANES), f32), ((16, inner), f32),
        ((1, LANES), f32), ((2 * LANES, inner), bf16), ((LANES, inner), bf16),
        ((D, 2 * STATE + LANES), bf16), ((CONV + 1, inner + 2 * STATE), f32), ((1, LANES), f32),
    ]
    return pl.pallas_call(
        functools.partial(prepare_kernel, heads, inner, blocks),
        out_shape=[
            (jax.ShapeDtypeStruct if k == 3 else far_memory)(*v) for k, v in enumerate(shapes)
        ],
        compiler_params=pltpu.CompilerParams(vmem_limit_bytes=VMEM),
        cost_estimate=LIGHT,
        name="prepare",
    )(log_decay_t, dt_t, bc_weight, conv_x, conv_bc, dt_bias, skip_gain)


def gather_kernel(
    owners, own, from_left, from_right, gain_0, gain_1, gain_2, w_0, w_1, w_2, o_0, o_1, o_2,
    acc, acc_others, squares, lhs,
):
    width = own.shape[1]
    square = None
    for k, (piece, gain) in enumerate(((own, gain_0), (from_left, gain_1), (from_right, gain_2))):
        values = piece[...].astype(f32)
        lhs[:, k * width : (k + 1) * width] = (values * gain[0]).astype(bf16)
        part = jnp.sum(values * values, axis=1, keepdims=True)
        square = part if square is None else square + part
    squares[...] = square
    acc[...] = jnp.dot(
        lhs[...], jnp.concatenate([w_0[0], w_1[0], w_2[0]], axis=0), preferred_element_type=f32
    )
    acc_others[...] = jnp.dot(
        lhs[...], jnp.concatenate([o_0[...], o_1[...], o_2[...]], axis=0), preferred_element_type=f32
    )


def gather(owners, own, from_left, from_right, gains, gate_x, others):
    rows, width = own.shape
    inner = gate_x.shape[2]
    narrow = others.shape[1]

    def whole(*shape):
        return pl.BlockSpec(shape, lambda n, o: (0,) * len(shape))

    def gain(k):
        return pl.BlockSpec((1, 1, width), lambda n, o: (o[k], 0, 0))

    def wide(k):
        return pl.BlockSpec((1, width, inner), lambda n, o: (1, o[k], 0))

    def small(k):
        return pl.BlockSpec((width, narrow), lambda n, o: (o[k], 0))

    return pl.pallas_call(
        gather_kernel,
        grid_spec=pltpu.PrefetchScalarGridSpec(
            num_scalar_prefetch=1,
            grid=(1,),
            in_specs=[whole(rows, width)] * 3 + [f(k) for f in (gain, wide, small) for k in range(3)],
            out_specs=[
                whole(rows, inner), whole(rows, narrow), whole(rows, 1),
            ],
            scratch_shapes=[pltpu.VMEM((rows, 3 * width), bf16)],
        ),
        out_shape=[
            far_memory((rows, inner), f32), far_memory((rows, narrow), f32), far_memory((rows, 1), f32),
        ],
        compiler_params=pltpu.CompilerParams(vmem_limit_bytes=VMEM),
        cost_estimate=LIGHT,
        name="gather",
    )(owners, own, from_left, from_right, gains, gains, gains, gate_x, gate_x, gate_x, others, others, others)


def gate_kernel(
    owners, own, from_left, from_right, far, gain_0, gain_1, gain_2, gain_3, w_0, w_1, w_2, w_3,
    squares, out, lhs,
):
    width = own.shape[1]
    for k, (piece, gain) in enumerate(
        ((own, gain_0), (from_left, gain_1), (from_right, gain_2), (far, gain_3))
    ):
        values = piece[...].astype(f32)
        lhs[:, k * width : (k + 1) * width] = (values * gain[0]).astype(bf16)
    square = squares[...] + jnp.sum(values * values, axis=1, keepdims=True)
    full = jnp.dot(
        lhs[...], jnp.concatenate([w_0[0], w_1[0], w_2[0], w_3[0]], axis=0), preferred_element_type=f32
    )
    out[...] = (full * lax.rsqrt(square * (1.0 / D) + eps)).astype(bf16)


def project_gate(rows, owners, pieces, gains, gate_x, squares):
    width = pieces[0].shape[1]
    inner = gate_x.shape[2]
    grid = rows // BLOCK

    def row(width):
        return pl.BlockSpec((BLOCK, width), lambda i, o: (i, 0))

    def gain(k):
        return pl.BlockSpec((1, 1, width), lambda i, o: (o[k], 0, 0))

    def wide(k):
        return pl.BlockSpec((1, width, inner), lambda i, o: (0, o[k], 0))

    return pl.pallas_call(
        gate_kernel,
        grid_spec=pltpu.PrefetchScalarGridSpec(
            num_scalar_prefetch=1,
            grid=(grid,),
            in_specs=[row(width)] * 4 + [f(k) for f in (gain, wide) for k in range(4)] + [row(1)],
            out_specs=row(inner),
            scratch_shapes=[pltpu.VMEM((BLOCK, 4 * width), bf16)],
        ),
        out_shape=far_memory((rows, inner), bf16),
        compiler_params=pltpu.CompilerParams(vmem_limit_bytes=VMEM),
        cost_estimate=LIGHT,
        name="gate",
    )(owners, *pieces, *[gains] * 4, *[gate_x] * 4, squares)


def front_kernel(
    inner, last,
    owner, acc, acc_others, piece, squares, gain, gate_x, others, near, taps, dt_bias, to_end, spread, keep, total,
    *rest,
):
    if last:
        later, join, x_out, bc_out, xs_out, entering, state, payload, extended, slabs = rest
    else:
        rim_acc, rim_others, rim_piece, rim_squares, x_out, bc_out, xs_out, entering, state, tail, extended = rest
    index = pl.program_id(0)
    wide = inner + 2 * STATE

    def scaled(piece):
        values = piece[...].astype(f32)
        return values, (values * gain[0]).astype(bf16)

    def row_scale(squares, values):
        square = squares[...] + jnp.sum(values * values, axis=1, keepdims=True)
        return lax.rsqrt(square * (1.0 / D) + eps)

    def dot(u, v):
        return jnp.dot(u, v, preferred_element_type=f32)

    @pl.when(index == 0)
    def _():
        state[...] = jnp.zeros_like(state)
        if last:
            extended[0:RIM] = near[...].astype(f32)
        else:
            values, lhs = scaled(rim_piece)
            scale = row_scale(rim_squares, values)
            x_rim = (rim_acc[...] + dot(lhs, gate_x[0])) * scale
            bc_rim = (
                rim_others[:, : 2 * STATE] + dot(lhs, others[:, : 2 * STATE])
            ) * scale
            extended[0:RIM, :inner] = x_rim.astype(bf16).astype(f32)
            extended[0:RIM, inner:] = bc_rim.astype(bf16).astype(f32)

    @pl.when(index > 0)
    def _():
        extended[0:RIM] = extended[BLOCK : BLOCK + RIM]

    values, lhs = scaled(piece)
    scale = row_scale(squares, values)
    x_raw = ((acc[...] + dot(lhs, gate_x[0])) * scale).astype(bf16)
    others_raw = ((acc_others[...] + dot(lhs, others[...])) * scale).astype(bf16)
    extended[RIM : RIM + BLOCK, :inner] = x_raw.astype(f32)
    extended[RIM : RIM + BLOCK, inner:] = others_raw[:, : 2 * STATE].astype(f32)
    step = jax.nn.softplus(others_raw[:, 2 * STATE :].astype(f32) + dt_bias[...])
    summed = taps[CONV : CONV + 1]
    for k in range(CONV):
        first = RIM - CONV + 1 + k
        summed = summed + taps[k : k + 1] * extended[first : first + BLOCK]
    conv = silu(summed)
    x_conv = conv[:, :inner].astype(bf16)
    bc = conv[:, inner:].astype(bf16)
    x_out[...] = x_conv
    bc_out[...] = bc
    x_wide = x_conv.astype(f32)
    by_step = dot(split(step), spread[...])
    by_end = dot(split(step * to_end[...]), spread[...])
    xs_out[...] = (x_wide * by_step).astype(bf16)
    weighted = (x_wide * by_end).astype(bf16)
    entering[0] = state[...]
    state[...] = keep[0] * state[...] + lax.dot_general(
        bc[:, :STATE], weighted, (((0,), (0,)), ((), ())), preferred_element_type=f32
    )

    @pl.when(index == pl.num_programs(0) - 1)
    def _():
        if last:
            half = STATE // 2
            chunks = inner // LANES
            joined = join[0] * state[...] + later[...]
            slabs[...] = jnp.zeros_like(slabs)
            for c in range(chunks):
                slabs[:, c] = joined[0:half, c * LANES : (c + 1) * LANES]
                slabs[:, chunks + c] = joined[half:STATE, c * LANES : (c + 1) * LANES]
            slabs[:, 2 * chunks] = jnp.broadcast_to(total[...], (half, LANES))
            payload[...] = slabs[...].astype(bf16)
        else:
            tail[...] = extended[BLOCK : BLOCK + RIM].astype(bf16)


def front(
    last, half, owner, acc, acc_others, piece, squares, gains, gate_x, others, near, taps, dt_bias, to_end,
    spread, keep, total, *more,
):
    width = piece.shape[1]
    inner = gate_x.shape[2]
    grid = to_end.shape[0] // BLOCK // 2
    rows = grid * BLOCK
    base = half * grid
    wide = inner + 2 * STATE
    pieces = STATE // 2

    def row(width, offset=0):
        return pl.BlockSpec((BLOCK, width), lambda i, o: (i + offset, 0))

    def whole(*shape):
        return pl.BlockSpec(shape, lambda i, o: (0,) * len(shape))

    def rim(width):
        return pl.BlockSpec((RIM, width), lambda i, o: (rows // RIM, 0))

    if last:
        operands = more
        extra = [whole(STATE, inner), pl.BlockSpec((1, 1, inner), lambda i, o: (9, 0, 0))]
        out_spec, out_shape = whole(pieces, 16, LANES), (pieces, 16, LANES)
        scratch = [pltpu.VMEM((pieces, 16, LANES), f32)]
    else:
        operands = (acc, acc_others, piece, squares)
        extra = [
            rim(inner), rim(acc_others.shape[1]), rim(width), rim(1),
        ]
        out_spec, out_shape = whole(RIM, wide), (RIM, wide)
        scratch = []
    return pl.pallas_call(
        functools.partial(front_kernel, inner, last),
        grid_spec=pltpu.PrefetchScalarGridSpec(
            num_scalar_prefetch=1,
            grid=(grid,),
            in_specs=[
                row(inner), row(acc_others.shape[1]),
                row(width), row(1),
                pl.BlockSpec((1, 1, width), lambda i, o: (o[0], 0, 0)),
                pl.BlockSpec((1, width, inner), lambda i, o: (1, o[0], 0)),
                pl.BlockSpec((width, others.shape[1]), lambda i, o: (o[0], 0)),
                whole(RIM, wide), whole(CONV + 1, wide),
                whole(1, LANES), row(LANES, base), whole(2 * LANES, inner),
                pl.BlockSpec((1, 1, inner), lambda i, o: (i + base, 0, 0)), whole(1, LANES),
            ] + extra,
            out_specs=[
                row(inner), row(2 * STATE), row(inner),
                pl.BlockSpec((1, STATE, inner), lambda i, o: (i, 0, 0)),
                whole(STATE, inner), out_spec,
            ],
            scratch_shapes=[pltpu.VMEM((BLOCK + RIM, wide), f32)] + scratch,
        ),
        out_shape=[
            far_memory((rows, inner), bf16),
            far_memory((rows, 2 * STATE), bf16),
            far_memory((rows, inner), bf16),
            far_memory((grid, STATE, inner), f32),
            far_memory((STATE, inner), f32),
            jax.ShapeDtypeStruct(out_shape, bf16),
        ],
        compiler_params=pltpu.CompilerParams(vmem_limit_bytes=VMEM),
        cost_estimate=LIGHT,
        name="front",
    )(owner, acc, acc_others, piece, squares, gains, gate_x, others, near, taps, dt_bias, to_end, spread, keep, total, *operands)


def scan_kernel(chunks, taken, spread, given, decays, sums):
    count = taken.shape[0]
    wide = taken[...].astype(f32)
    decays[...] = wide
    rows = decays[:, 2 * chunks]
    gains = jnp.exp(jnp.dot(rows.astype(bf16), spread[...], preferred_element_type=f32))
    sums[...] = wide
    decays[...] = jnp.zeros_like(decays)
    for c in range(chunks):
        part = gains[:, c * LANES : (c + 1) * LANES]
        decays[:, c] = part
        decays[:, chunks + c] = part
    running = jnp.zeros(taken.shape[1:], f32)
    for j in range(count):
        following = decays[j] * running + sums[j]
        sums[j] = running
        running = following
    given[...] = sums[...].astype(bf16)


def scan(taken, spread):
    chunks = spread.shape[1] // LANES
    return pl.pallas_call(
        functools.partial(scan_kernel, chunks),
        out_shape=jax.ShapeDtypeStruct(taken.shape, bf16),
        scratch_shapes=[pltpu.VMEM(taken.shape, f32), pltpu.VMEM(taken.shape, f32)],
        compiler_params=pltpu.CompilerParams(vmem_limit_bytes=VMEM // 2),
        cost_estimate=LIGHT,
        name="scan",
    )(taken, spread)


def inside_kernel(heads, bc, xs, decay, decay_t, out):
    both = bc[...]
    scores = lax.dot_general(
        both[:, STATE:], both[:, :STATE], (((1,), (1,)), ((), ())), preferred_element_type=f32
    )
    row = lax.broadcasted_iota(jnp.int32, (BLOCK, BLOCK), 0)
    column = lax.broadcasted_iota(jnp.int32, (BLOCK, BLOCK), 1)
    scores = jnp.where(row >= column, scores, 0.0)
    sums = decay[...]
    first = lax.broadcasted_iota(jnp.int32, (BLOCK, LANES), 1) < HEADDIM
    for pair in range(heads // 2):
        span = slice(pair * LANES, (pair + 1) * LANES)
        found = []
        for h in (2 * pair, 2 * pair + 1):
            gap = jnp.minimum(sums[:, h : h + 1] - decay_t[h : h + 1, :], 0.0)
            mix = (scores * jnp.exp(gap)).astype(bf16)
            found.append(jnp.dot(mix, xs[:, span], preferred_element_type=f32))
        out[:, span] = jnp.where(first, found[0], found[1])


def inside(bc, xs, decay, decay_t, half):
    rows, inner = xs.shape
    grid = rows // BLOCK
    base = half * grid
    return pl.pallas_call(
        functools.partial(inside_kernel, inner // HEADDIM),
        grid=(grid,),
        in_specs=[
            pl.BlockSpec((BLOCK, 2 * STATE), lambda i: (i, 0)),
            pl.BlockSpec((BLOCK, inner), lambda i: (i, 0)),
            pl.BlockSpec((BLOCK, LANES), lambda i: (i + base, 0)),
            pl.BlockSpec((16, BLOCK), lambda i: (0, i + base)),
        ],
        out_specs=pl.BlockSpec((BLOCK, inner), lambda i: (i, 0)),
        out_shape=far_memory((rows, inner), f32),
        compiler_params=pltpu.CompilerParams(vmem_limit_bytes=VMEM),
        cost_estimate=LIGHT,
        name="inside",
    )(bc, xs, decay, decay_t)


def tail_kernel(
    inner, half_index,
    y_in, x_conv, gate, bc, entering, taken, earlier, fade_in, before, skip, decay, spread, gain, weight,
    far, scaled_out, squares, slabs, incoming,
):
    chunks = inner // LANES

    @pl.when(pl.program_id(0) == 0)
    def _():
        squares[...] = jnp.zeros_like(squares)
        slabs[...] = taken[...].astype(f32)
        half = STATE // 2
        for c in range(chunks):
            incoming[0:half, c * LANES : (c + 1) * LANES] = slabs[:, c]
            incoming[half:STATE, c * LANES : (c + 1) * LANES] = slabs[:, chunks + c]
        if half_index:
            incoming[...] = earlier[...] + fade_in[0] * incoming[...]

    carried = (entering[0] + before[0] * incoming[...]).astype(bf16)
    fade = jnp.dot(split(jnp.exp(decay[...])), spread[...], preferred_element_type=f32)
    y = y_in[...] + fade * jnp.dot(bc[:, STATE:], carried, preferred_element_type=f32)
    y = y + skip[0] * x_conv[...].astype(f32)
    gated = y * silu(gate[...].astype(f32))
    step = pl.program_id(0)
    square = jnp.sum(gated * gated, axis=1, keepdims=True)
    squares[pl.ds(step, 1)] = jnp.transpose(jnp.broadcast_to(square, (BLOCK, LANES)))[:1]
    scaled = (gated * gain[...]).astype(bf16)
    width = far.shape[1]
    place = pl.ds(pl.multiple_of(step * BLOCK, BLOCK), BLOCK)
    far[place] = jnp.dot(scaled, weight[...], preferred_element_type=f32).astype(bf16)
    scaled_out[place] = scaled

    @pl.when(step == pl.num_programs(0) - 1)
    def _():
        rows = far.shape[0] - 16
        parts = coded(squares[...])
        for out in (far, scaled_out):
            out[rows : rows + 16, :BLOCK] = parts
            out[rows : rows + 16, BLOCK:] = jnp.zeros((16, out.shape[1] - BLOCK), bf16)


def tail(half, y_in, x_conv, gate, bc, entering, taken, earlier, channels, decay, spread, gain, weight):
    rows, inner = y_in.shape
    grid = rows // BLOCK
    base = half * grid
    blocks = 2 * grid

    def channel(first, stride=0):
        return pl.BlockSpec((1, 1, inner), lambda i: (first + stride * i, 0, 0))

    width = weight.shape[1] // 4

    def row(width, offset=0):
        return pl.BlockSpec((BLOCK, width), lambda i: (i + offset, 0))

    def whole(*shape):
        return pl.BlockSpec(shape, lambda i: (0,) * len(shape))

    return pl.pallas_call(
        functools.partial(tail_kernel, inner, half),
        grid=(grid,),
        in_specs=[
            row(inner), row(inner), row(inner), row(2 * STATE),
            pl.BlockSpec((1, STATE, inner), lambda i: (i, 0, 0)),
            whole(*taken.shape), whole(STATE, inner), channel(2 * blocks), channel(blocks + base, 1),
            channel(2 * blocks + 2), row(LANES, base), whole(2 * LANES, inner), whole(1, inner),
            pl.BlockSpec((inner, width), lambda i: (0, 2)),
        ],
        out_specs=[whole(rows + 16, width), whole(rows + 16, inner)],
        out_shape=[far_memory((rows + 16, width), bf16), far_memory((rows + 16, inner), bf16)],
        scratch_shapes=[
            pltpu.VMEM((8, BLOCK), f32), pltpu.VMEM(taken.shape, f32), pltpu.VMEM((STATE, inner), f32),
        ],
        compiler_params=pltpu.CompilerParams(vmem_limit_bytes=VMEM),
        cost_estimate=pl.CostEstimate(
            flops=2 * rows * inner * (weight.shape[1] + STATE),
            bytes_accessed=rows * inner * 10 + weight.size * 2, transcendentals=rows * inner,
        ),
        name="tail",
    )(
        y_in, x_conv, gate, bc, entering, taken, earlier, channels, channels, channels, decay, spread, gain,
        weight,
    )


def rest_kernel(scaled_b, scaled_a, weight, right_b, left_b, own_b, left_a, right_a, own_a):
    width = own_a.shape[1]
    for scaled, outs in ((scaled_b, (own_b, right_b, left_b)), (scaled_a, (own_a, right_a, left_a))):
        rows = scaled.shape[0] - 16
        for n, out in zip((0, 1, 3), outs):
            out[:rows] = jnp.dot(
                scaled[:rows], weight[:, n * width : (n + 1) * width], preferred_element_type=f32
            ).astype(bf16)
            out[rows:] = scaled[rows:, :width]


def rest(scaled_b, scaled_a, weight):
    shape = jax.ShapeDtypeStruct((scaled_a.shape[0], weight.shape[1] // 4), bf16)
    return pl.pallas_call(
        rest_kernel,
        out_shape=[shape] * 6,
        compiler_params=pltpu.CompilerParams(vmem_limit_bytes=VMEM),
        cost_estimate=pl.CostEstimate(
            flops=3 * scaled_a.size * weight.shape[1], bytes_accessed=4 * scaled_a.size + 2 * weight.size,
            transcendentals=0,
        ),
        name="rest",
    )(scaled_b, scaled_a, weight)


def add_kernel(u, v, out):
    rows = out.shape[0] - 16
    out[:rows] = (u[:rows].astype(f32) + v[:rows].astype(f32)).astype(bf16)
    out[rows:] = coded(decoded(u[rows:]) + decoded(v[rows:]))


def add(u, v):
    return pl.pallas_call(
        add_kernel, out_shape=jax.ShapeDtypeStruct(u.shape, bf16), cost_estimate=LIGHT, name="add",
        compiler_params=pltpu.CompilerParams(vmem_limit_bytes=VMEM // 2),
    )(u, v)


def finish_kernel(own_a, direct_a, arrived_a, own_b, direct_b, arrived_b, out):
    rows = own_a.shape[0] - 16
    for h, parts in enumerate(((own_a, direct_a, arrived_a), (own_b, direct_b, arrived_b))):
        squares = sum(decoded(p[rows:, :BLOCK]) for p in parts)
        scales = jnp.transpose(lax.rsqrt(squares * (1.0 / INNER) + eps))
        for k in range(rows // BLOCK):
            span = slice(k * BLOCK, (k + 1) * BLOCK)
            total = sum(p[span].astype(f32) for p in parts)
            first = h * rows + k * BLOCK
            out[first : first + BLOCK] = (total * scales[:, k : k + 1]).astype(bf16)


def finish(*parts):
    rows, width = parts[0].shape
    return pl.pallas_call(
        finish_kernel, out_shape=jax.ShapeDtypeStruct((2 * (rows - 16), width), bf16),
        compiler_params=pltpu.CompilerParams(vmem_limit_bytes=VMEM // 2),
        cost_estimate=LIGHT, name="finish",
    )(*parts)


def per_device(
    hidden, norm_gain, zx_weight, bc_weight, dt_weight, conv_x, conv_bc, dt_bias,
    log_decay, skip_gain, out_gain, out_weight,
):
    rows, width = hidden.shape
    heads = dt_weight.shape[1]
    inner = zx_weight.shape[2]
    blocks = rows // BLOCK
    middle = rows // 2
    groups = lax.axis_size("head")
    places = lax.axis_size("ctx")
    me = lax.axis_index("head")
    to_right = [(i, (i + 1) % groups) for i in range(groups)]
    to_left = [(i, (i - 1) % groups) for i in range(groups)]

    def right(v):
        return lax.ppermute(v, "head", to_right)

    def left(v):
        return lax.ppermute(v, "head", to_left)

    bottom = jnp.concatenate([hidden[middle:], hidden[middle - RIM : middle]], axis=0)
    right_bottom, left_bottom = right(bottom), left(bottom)
    gate_x = jnp.transpose(zx_weight, (1, 0, 2))
    gains = norm_gain.reshape(groups, 1, width)
    owners = jnp.stack([me, lax.rem(me + groups - 1, groups), lax.rem(me + 1, groups)]).astype(jnp.int32)
    owner = lax.rem(me + 2, groups).astype(jnp.int32)[None]
    all_owners = jnp.concatenate([owners, owner])
    prepared = prepare(
        *kept(
            jnp.transpose(log_decay), jnp.transpose(dt_weight), bc_weight, conv_x, conv_bc,
            dt_bias[None], skip_gain[None],
        )
    )
    right_bottom, hidden, gate_x, prepared = lax.optimization_barrier(
        (right_bottom, hidden, gate_x, prepared)
    )
    decay, decay_t, to_end, channels, total, spread, thrice, others, taps, bias = prepared
    gate_x, = kept(gate_x)
    far_bottom = right(right_bottom)
    top = hidden[:middle]
    left_top = left(top)
    acc_b, others_b, squares_b = gather(owners, bottom, right_bottom, left_bottom, gains, gate_x, others)
    left_top, acc_b, top = lax.optimization_barrier((left_top, acc_b, top))
    far_top = left(left_top)
    right_top = right(top)

    channels = channels[:, None]
    gain = out_gain[None]

    no_rim = jnp.zeros((RIM, inner + 2 * STATE), bf16)
    x_b, bc_b, xs_b, enter_b, state_b, raw_tail = front(
        False, 1, owner, *kept(acc_b, others_b), far_bottom, *kept(squares_b), gains, gate_x, others, no_rim, taps,
        bias, *kept(to_end), spread, channels, total,
    )
    near = lax.ppermute(raw_tail, "ctx", [(i, i + 1) for i in range(places - 1)])
    acc_a, others_a, squares_a = gather(owners, top, right_top, left_top, gains, gate_x, others)
    x_a, bc_a, xs_a, enter_a, state_a, payload = front(
        True, 0, owner, *kept(acc_a, others_a), far_top, *kept(squares_a), gains, gate_x, others, near, taps, bias,
        *kept(to_end), spread, channels, total, state_b, channels,
    )
    taken = lax.all_to_all(payload, "ctx", 0, 0)
    inside_a = inside(*kept(bc_a, xs_a, decay, decay_t), 0)
    turned = jnp.concatenate(
        [
            lax.dynamic_slice_in_dim(out_weight, lax.rem(me + k, groups) * width, width, 1)
            for k in range(groups)
        ],
        axis=1,
    )
    gate_a = project_gate(
        middle, all_owners, kept(top, right_top, left_top, far_top), gains, gate_x, *kept(squares_a)
    )
    taken, inside_a, turned, gate_a = lax.optimization_barrier((taken, inside_a, turned, gate_a))
    incoming = lax.all_to_all(scan(taken, *kept(thrice)), "ctx", 0, 0)
    inside_b = inside(*kept(bc_b, xs_b, decay, decay_t), 1)
    gate_b = project_gate(
        middle, all_owners, kept(bottom, right_bottom, left_bottom, far_bottom), gains, gate_x,
        *kept(squares_b),
    )
    incoming, inside_b, gate_b = lax.optimization_barrier((incoming, inside_b, gate_b))

    far_b, scaled_b = tail(
        1, *kept(inside_b, x_b, gate_b, bc_b, enter_b), incoming, *kept(state_a), channels, decay,
        spread, gain, turned,
    )
    far_a, scaled_a = tail(
        0, *kept(inside_a, x_a, gate_a, bc_a, enter_a), incoming, state_a, channels, decay, spread,
        gain, turned,
    )
    passed_b = left(far_b)
    passed_a = right(far_a)
    right_b, left_b, own_b, left_a, right_a, own_a = rest(scaled_b, scaled_a, turned)
    direct_a, direct_b = left(left_a), right(right_b)
    arrived_a = right(add(right_a, passed_a))
    arrived_b = left(add(left_b, passed_b))
    return finish(own_a, direct_a, arrived_a, own_b, direct_b, arrived_b)


def solution(mesh):
    placed = (
        P("ctx", "head"), P(), P(None, None, "head"), P(), P(None, "head"), P(None, "head"), P(),
        P("head"), P("ctx", "head"), P("head"), P("head"), P("head", None),
    )
    return jax.shard_map(
        per_device, mesh=mesh, in_specs=placed, out_specs=P("ctx", "head"), check_vma=False
    )
```
